128 devices in a mesh: dp: 64 (over z, y, x), rep: 2 (over core).
Axes of the slice: x: 4, y: 4, z: 4, core: 2. Of those that a mesh axis runs over, the one named last changes fastest.
Arguments:
- rows_in: bfloat16 [262144, 512], P(('dp', 'rep')), may hold values from -6 to 6
- row_codes: int32 [262144], P(('dp', 'rep')), may hold values from 0 to 8191, as said below
- hot_split: int32 [256, 2], replicated, may hold values from 0 to 8191, as said below
- codebook: float32 [8192, 512], P('dp'), may hold values from -6 to 6
Outputs:
- new_codebook: float32 [8192, 512], P(('dp', 'rep'))
- next_residual: bfloat16 [262144, 512], P(('dp', 'rep'))
The draws below stay inside these ranges and needn't reach their ends.
Inputs may be any that keep to these rules, and one draw needn't show every extreme that they name: `row_codes`: among the rows of one device, at most 48 have codes (after the split) in any one owner block codes // 128; in every draw some owner block receives exactly 48 rows from every device. `hot_split`: the hot ids are distinct; each partner differs from its hot id and lies in the same owner block (id // 128).
All inputs are finite; a program needn't handle non-finite values.
Results may differ from the reference program's by a relative error of at most 0.0055.
Values may be sent and summed in bfloat16 or wider, within the bound.
A program may use at most 64 MiB of HBM per device.

```python
import jax
import jax.numpy as jnp

E = 512
K = 8192
H = 256
ROW_DEV = 2048
ROWS = 262144
KB = 128
N_DP = 64


def draw_row_codes(key, part):
    key = jax.random.fold_in(key, 11)
    owners_count = N_DP
    per_owner = ROW_DEV // owners_count
    biggest = per_owner + per_owner // 2
    pattern = jnp.arange(owners_count, dtype=jnp.int32) % 4
    base_counts = jnp.where(pattern == 0, biggest, jnp.where(pattern == 1, per_owner - per_owner // 2, per_owner)).astype(jnp.int32)
    shared_key, rest_key = jax.random.split(key)
    full_owner = jax.random.randint(shared_key, (), 0, owners_count)
    device_count = ROWS // ROW_DEV
    device_keys = jax.random.split(rest_key, device_count)

    def one_device(dev_key):
        key_a, key_b, key_c = jax.random.split(dev_key, 3)
        counts = base_counts[jax.random.permutation(key_a, owners_count)]
        where_full = jnp.argmax((counts == biggest).astype(jnp.int32))
        value_there = counts[full_owner]
        counts = counts.at[where_full].set(value_there)
        counts = counts.at[full_owner].set(biggest)
        owners = jnp.repeat(jnp.arange(owners_count, dtype=jnp.int32), counts, total_repeat_length=ROW_DEV)
        owners = owners[jax.random.permutation(key_b, ROW_DEV)]
        within = jax.random.randint(key_c, (ROW_DEV,), 0, KB)
        return (owners * KB + within).astype(jnp.int32)
    return jax.vmap(one_device)(device_keys).reshape(-1).astype(jnp.int32)


def draw_hot_split(key, part):
    key = jax.random.fold_in(key, 23)
    key_a, key_b = jax.random.split(key)
    hot_ids = jax.random.permutation(key_a, K)[:H].astype(jnp.int32)
    shift = jax.random.randint(key_b, (H,), 1, KB)
    partner = hot_ids // KB * KB + (hot_ids % KB + shift) % KB
    return jnp.stack([hot_ids, partner.astype(jnp.int32)], axis=1).astype(jnp.int32)


def steps_of(key, extent, shards, smallest, top_value):
    gain, own = 1.0, jax.random.fold_in(key, 6)
    for position, blocks in shards:
        heights = jnp.exp(jax.random.uniform(jax.random.fold_in(own, position), (blocks,), jnp.float32, smallest / len(shards), top_value / len(shards)))
        gain = gain * jnp.repeat(heights, extent[position] // blocks).reshape([-1 if axis == position else 1 for axis in range(len(extent))])
    return gain


def centred(rng, dims, spread, reach, cuts=(), kind=jnp.bfloat16):
    entries = spread * jax.random.normal(rng, dims, jnp.float32)
    if cuts:
        entries = entries * steps_of(rng, dims, cuts, -0.22, 0.18)
    return jnp.clip(entries, -reach, reach).astype(kind)


def setup_inputs(seed: int = 0) -> dict:
    keys = jax.random.split(jax.random.key(seed), 5)
    return {
        "rows_in": centred(keys[0], (ROWS, E), 1.0, 6.0, ((0, 128),)),
        "row_codes": draw_row_codes(jax.random.fold_in(keys[4], 71), 0),
        "hot_split": draw_hot_split(jax.random.fold_in(keys[4], 71), 0),
        "codebook": centred(keys[3], (K, E), 1.0, 6.0, ((0, 64),), jnp.float32),
    }


prior_weight = 8.0


def split_codes(row_codes, hot_split):
    row_number = jnp.arange(row_codes.shape[0], dtype=jnp.int32)
    is_odd = (row_number % 2) == 1
    matched = row_codes[:, None] == hot_split[None, :, 0]
    is_hot = jnp.any(matched, axis=1)
    partner = jnp.sum(jnp.where(matched, hot_split[None, :, 1], 0), axis=1).astype(jnp.int32)
    return jnp.where(is_odd & is_hot, partner, row_codes).astype(jnp.int32)


def reference(rows_in, row_codes, hot_split, codebook):
    codes = split_codes(row_codes, hot_split)
    rows_wide = rows_in.astype(jnp.float32)
    code_sums = jax.ops.segment_sum(rows_wide, codes, num_segments=K)
    code_counts = jax.ops.segment_sum(jnp.ones((codes.shape[0],), jnp.float32), codes, num_segments=K)
    new_codebook = (code_sums + prior_weight * codebook) / (code_counts[:, None] + prior_weight)
    table_low = new_codebook.astype(jnp.bfloat16)
    picked = table_low[codes].astype(jnp.float32)
    next_residual = (rows_wide - picked).astype(jnp.bfloat16)
    return new_codebook, next_residual
```

```python
import jax
import jax.numpy as jnp
from jax import lax
from jax.experimental import pallas as pl
from jax.experimental.pallas import tpu as pltpu
from jax.sharding import PartitionSpec as P

MESH = pl.DeviceIdType.MESH
F32, BF16, I32 = jnp.float32, jnp.bfloat16, jnp.int32

PRIOR = 8.0
ROWS = 2048
E = 512
KB = 128
OWNERS = 64
SLOTS = 48
PITCH = 64
GROUP = 8
GS = GROUP * SLOTS
NG = OWNERS // GROUP
LANES = ROWS // 128

WIDTH = (256, 128, 128)
COL = (0, 256, 384)
CUT = ((0, 48), (48, 48), (96, 32))

NT = (((1,), (1,)), ((), ()))


def iota(shape, dim):
    return lax.broadcasted_iota(I32, shape, dim)


def kernel(rows, codes, hot, cb, newcb, res, pk, r1, crow, s2, acc2, r2, s3, acc3, r3, tb,
           rowbuf, vcol, sc_send, sc_recv, cn1, cr1, cn2, cr2, cn3, cr3, cx, cxr,
           tot3, tot3r, nb, nbr, slot, picks, psend,
           rs_s, rs_r, sc_s, sc_r, cn_s, cn_r, ag_s, ag_r, x_s, x_r, p_s, p_r):
    d = lax.axis_index("dp")
    r = lax.axis_index("rep")
    x, y, z = lax.rem(d, 4), lax.rem(d // 4, 4), d // 16
    mine = (x, y, z)
    stride = (1, 4, 16)
    sibling = (d, 1 - r)

    def pick(seq, u, stage):
        a, b = seq[(u + stage) % 3], seq[(u + stage + 1) % 3]
        return a + r * (b - a)

    def digits(coords, u):
        return tuple(pick(coords, u, stage) for stage in range(3))

    def peer(u, stage, k):
        c = pick(mine, u, stage)
        there = lax.rem(c + k, 4)
        return (d + (there - c) * pick(stride, u, stage), r), there

    my_digits = [digits(mine, u) for u in range(3)]

    barrier = pltpu.get_barrier_semaphore()
    for axis in range(3):
        for k in range(1, 4):
            there = lax.rem(mine[axis] + k, 4)
            pl.semaphore_signal(barrier, inc=1, device_id=(d + (there - mine[axis]) * stride[axis], r),
                                device_id_type=MESH)
    pl.semaphore_signal(barrier, inc=1, device_id=sibling, device_id_type=MESH)

    hot_id = jnp.broadcast_to(hot[:, 0:1], (256, 128))
    hot_to = jnp.broadcast_to(hot[:, 1:2] + 1, (256, 128)).astype(F32)
    odd = lax.rem(iota((1, 128), 1), 2) == 1
    before = jnp.where(iota((128, 128), 0) < iota((128, 128), 1), 1.0, 0.0).astype(BF16)
    owner_id = iota((OWNERS, 128), 0)
    carry = jnp.zeros((OWNERS, 128), F32)
    for b in range(LANES):
        lanes = slice(b * 128, (b + 1) * 128)
        code = codes[b:b + 1, :]
        partner = jnp.sum(jnp.where(hot_id == code, hot_to, 0.0), axis=0, keepdims=True)
        code = jnp.where(odd & (partner > 0.0), partner.astype(I32) - 1, code)
        owner = code // KB
        mark = jnp.where(owner_id == owner, 1.0, 0.0)
        ahead = jnp.dot(mark.astype(BF16), before, preferred_element_type=F32) + carry
        rank = jnp.sum(mark * ahead, axis=0, keepdims=True)
        carry = carry + jnp.sum(mark, axis=1, keepdims=True)
        owner_f = owner.astype(F32)
        rowbuf[0:1, lanes] = owner_f * SLOTS + rank
        rowbuf[1:2, lanes] = owner_f
        rowbuf[2:3, lanes] = rank
        rowbuf[3:4, lanes] = (code - owner * KB).astype(F32)

    for u in range(3):
        r1[u][:, :, SLOTS:, :] = jnp.zeros((16, 4, PITCH - SLOTS, WIDTH[u]), BF16)

    one, zero = jnp.ones((), BF16), jnp.zeros((), BF16)
    slot_iota = (iota((GS, 128), 0) - GS // 2).astype(F32).astype(BF16)

    def slot_rows(group):
        middle = (group * GS + GS // 2).astype(F32)
        tiles = []
        for b in range(LANES):
            v = jnp.broadcast_to(rowbuf[0:1, b * 128:(b + 1) * 128] - middle, (16, 128)).astype(BF16)
            v = jnp.concatenate([v] * (GS // 16), axis=0)
            tiles.append(jnp.where(v == slot_iota, one, zero))
        return jnp.concatenate(tiles, axis=1)

    pl.semaphore_wait(barrier, 10)

    def pack(step, _):
        oz = lax.rem(z + 1 + step // 2, 4)
        half = lax.rem(step, 2)
        packed = jnp.dot(slot_rows(oz * 2 + half), rows[...], preferred_element_type=F32).astype(BF16)
        for j in range(GROUP):
            where = (j % 4, half * 2 + j // 4, oz)
            for u in range(3):
                c1, c2, c3 = digits(where, u)
                at, sub = c1 * 16 + c2 * 4 + c3, c2 * 4 + c3
                k = lax.rem(c1 - my_digits[u][0] + 4, 4)
                pk[u][at] = packed[j * SLOTS:(j + 1) * SLOTS, COL[u]:COL[u] + WIDTH[u]]
                src, dst = pk[u].at[at], r1[u].at[sub, k, pl.ds(0, SLOTS)]

                @pl.when(k == 0)
                def _():
                    pltpu.make_async_copy(src, dst, rs_r.at[u, 0, 0]).start()

                @pl.when(k != 0)
                def _():
                    to = (d + (c1 - my_digits[u][0]) * pick(stride, u, 0), r)
                    pltpu.make_async_remote_copy(src, dst, rs_s.at[u, 0, k], rs_r.at[u, 0, k], device_id=to,
                                                 device_id_type=MESH).start()
        return 0

    lax.fori_loop(0, NG, pack, 0)

    o = rowbuf[1:2, :].astype(I32)
    coords = (lax.rem(o, 4), lax.rem(o // 4, 4), o // 16)

    def lane_tiles(f):
        return jnp.concatenate([f(slice(b * 128, (b + 1) * 128)) for b in range(LANES)], axis=1)

    id128 = iota((128, 128), 0).astype(F32)
    rank_mark = lane_tiles(lambda s: jnp.where(rowbuf[2:3, s] == id128, 1.0, 0.0).astype(BF16))
    low_mark = lane_tiles(lambda s: jnp.where(rowbuf[3:4, s] == id128, 1.0, 0.0).astype(BF16))

    def small_copy(src, dst, ss, rs, to):
        return pltpu.make_async_remote_copy(src, dst, ss, rs, device_id=to, device_id_type=MESH)

    sc_copies, cn_copies = {}, {}
    for u in range(3):
        c1, c2, c3 = digits(coords, u)
        place = c1 * 16 + c2 * 4 + c3
        low = lane_tiles(lambda s: jnp.where(place[:, s] == owner_id, rowbuf[3:4, s] + 1.0, 0.0).astype(BF16))
        sc = lax.dot_general(low, rank_mark, NT, preferred_element_type=F32).astype(BF16)
        for c in range(4):
            sc_send[u, c] = sc[c * 16:(c + 1) * 16]
        for k in range(1, 4):
            to, there = peer(u, 0, k)
            sc_copies[u, k] = small_copy(sc_send.at[u, there], sc_recv.at[u, k], sc_s.at[u, k], sc_r.at[u, k], to)
            sc_copies[u, k].start()
        if u == 0:
            own = lane_tiles(lambda s: jnp.where(place[:, s] == owner_id, 1.0, 0.0).astype(BF16))
            cn = lax.dot_general(own, low_mark, NT, preferred_element_type=F32)
            for c in range(4):
                cn1[c] = cn[c * 16:(c + 1) * 16]
            for k in range(1, 4):
                to, there = peer(0, 0, k)
                cn_copies[0, k] = small_copy(cn1.at[there], cr1.at[k], cn_s.at[0, k], cn_r.at[0, k], to)
                cn_copies[0, k].start()

    low_wide = lane_tiles(
        lambda s: jnp.concatenate([jnp.broadcast_to(rowbuf[3:4, s] + 1.0, (16, 128)).astype(BF16)] * 8, axis=0))

    def slot_code(g, _):
        slot[0, pl.ds(g * GS, GS)] = lax.dot_general(
            slot_rows(g), low_wide, NT, preferred_element_type=F32).astype(BF16)
        return 0

    lax.fori_loop(0, NG, slot_code, 0)
    slot_copy = small_copy(slot.at[0], slot.at[1], x_s.at[3], x_r.at[3], sibling)
    slot_copy.start()
    for b in range(LANES):
        v = jnp.broadcast_to(rowbuf[0:1, b * 128:(b + 1) * 128], (128, 128))
        vcol[b * 128:(b + 1) * 128, :] = jnp.transpose(v)

    code_id = (iota((KB, 256), 0) + 1).astype(F32)
    s1_copies, s2_copies, s3_copies = {}, {}, {}
    for u in range(3):
        for k in range(1, 4):
            to, there = peer(u, 0, k)
            s1_copies[u, k] = pltpu.make_async_remote_copy(
                pk[u].at[pl.ds(there * 16, 16)], r1[u].at[:, k, pl.ds(0, SLOTS)], rs_s.at[u, 0, k],
                rs_r.at[u, 0, k], device_id=to, device_id_type=MESH)
    for u in (1, 2, 0):
        c1, c2, c3 = my_digits[u]
        pltpu.make_async_copy(pk[u].at[pl.ds(c1 * 16, 16)], r1[u].at[:, 0, pl.ds(0, SLOTS)],
                              rs_r.at[u, 0, 0]).wait()
        for k in range(1, 4):
            s1_copies[u, k].wait_recv()
            sc_copies[u, k].wait_recv()
        quarter = [sc_send[u, c1].astype(F32)] + [sc_recv[u, k].astype(F32) for k in range(1, 4)]
        crow[u, :, 0:128] = quarter[0] + pltpu.roll(quarter[1], 64, 1)
        crow[u, :, 128:256] = quarter[2] + pltpu.roll(quarter[3], 64, 1)
        for q in (1, 3, 2, 0):
            to, there = peer(u, 1, q)
            for t in range(4):
                j = there * 4 + t
                mark = jnp.where(code_id == crow[u, pl.ds(j, 1), :], 1.0, 0.0).astype(BF16)
                part = jnp.dot(mark, r1[u][j].reshape(4 * PITCH, WIDTH[u]), preferred_element_type=F32)
                if q == 0:
                    acc2[u][t] = part
                else:
                    s2[u][q - 1, t] = part.astype(BF16)
            if q:
                s2_copies[u, q] = small_copy(s2[u].at[q - 1], r2[u].at[q - 1], rs_s.at[u, 1, q], rs_r.at[u, 1, q], to)
                s2_copies[u, q].start()
        if u == 0:
            total = cn1[c1]
            for k in range(1, 4):
                cn_copies[0, k].wait_recv()
                total = total + cr1[k]
            cn2[...] = total
            for k in range(1, 4):
                cn_copies[1, k] = small_copy(cn2, cr2.at[k - 1], cn_s.at[1, k], cn_r.at[1, k], peer(0, 1, k)[0])
                cn_copies[1, k].start()

    for u in (1, 2, 0):
        for q in range(1, 4):
            s2_copies[u, q].wait_recv()
        for q in (1, 3, 2, 0):
            to, there = peer(u, 2, q)
            part = acc2[u][there]
            for k in range(3):
                part = part + r2[u][k, there].astype(F32)
            if q == 0:
                acc3[u][...] = part
            else:
                s3[u][q - 1] = part.astype(BF16)
                s3_copies[u, q] = small_copy(s3[u].at[q - 1], r3[u].at[q - 1], rs_s.at[u, 2, q], rs_r.at[u, 2, q], to)
                s3_copies[u, q].start()
        if u == 0:
            total = cn2[...]
            for k in range(1, 4):
                cn_copies[1, k].wait_recv()
                total = total + cr2[k - 1]
            cn3[...] = total
            for k in range(1, 4):
                cn_copies[2, k] = small_copy(cn3, cr3.at[k - 1], cn_s.at[2, k], cn_r.at[2, k], peer(0, 2, k)[0])
                cn_copies[2, k].start()

    for u in (1, 2, 0):
        part = acc3[u][...]
        for q in range(1, 4):
            s3_copies[u, q].wait_recv()
            part = part + r3[u][q - 1].astype(F32)
        if u == 0:
            tot3[0] = part
        else:
            tot3[1, :, (u - 1) * 128:u * 128] = part
    total = cn3[...]
    for k in range(1, 4):
        cn_copies[2, k].wait_recv()
        total = total + cr3[k - 1]
    mine_at = my_digits[0][1] * 4 + my_digits[0][2]
    cx[...] = jnp.broadcast_to(
        jnp.sum(jnp.where(iota((16, 128), 0) == mine_at, total, 0.0), axis=0, keepdims=True), (8, 128))
    tot_copy = small_copy(tot3.at[1 - r], tot3r, x_s.at[0], x_r.at[0], sibling)
    cx_copy = small_copy(cx, cxr, x_s.at[1], x_r.at[1], sibling)
    cx_copy.start()
    tot_copy.start()
    cx_copy.wait_recv()
    count = cx[0:1, :] + cxr[0:1, :]
    diagonal = iota((128, 128), 0) == iota((128, 128), 1)
    count = jnp.sum(jnp.where(diagonal, jnp.broadcast_to(count, (128, 128)), 0.0), axis=1, keepdims=True)
    old = jnp.where(r == 0, cb[:, :256], cb[:, 256:])
    tot_copy.wait_recv()
    new = (tot3[r] + tot3r[...] + PRIOR * old) / (count + PRIOR)
    low_new = new.astype(BF16)
    ag = {}
    for u in range(3):
        c1, c2, c3 = my_digits[u]
        tb[u][c1 * 16 + c2 * 4 + c3] = low_new[CUT[u][0]:CUT[u][0] + CUT[u][1]]

    for stage, size in ((2, 1), (1, 4), (0, 16)):
        for u in range(3):
            c1, c2, c3 = my_digits[u]
            first = c1 * 16 + (c2 * 4 if size < 16 else 0) + (c3 if size < 4 else 0)
            block = tb[u].at[pl.ds(first, size)]
            if stage < 2:
                for k in range(1, 4):
                    ag[u, stage + 1, k].wait_recv()
            for k in range(1, 4):
                ag[u, stage, k] = small_copy(block, block, ag_s.at[u, stage, k], ag_r.at[u, stage, k],
                                             peer(u, stage, k)[0])
                ag[u, stage, k].start()
        if stage == 2:
            nb[0] = new[:64]
            nb[1] = new[64:]
            new_copy = small_copy(nb.at[1 - r], nbr, x_s.at[2], x_r.at[2], sibling)
            new_copy.start()
    new_copy.wait_recv()
    kept = nb[r]
    newcb[:, :256] = jnp.where(r == 0, kept, nbr[...])
    newcb[:, 256:] = jnp.where(r == 0, nbr[...], kept)
    slot_copy.wait_recv()
    for u in range(3):
        for k in range(1, 4):
            ag[u, 0, k].wait_recv()

    lane_code = (iota((SLOTS, 128), 1) + 1).astype(F32).astype(BF16)

    def take(g, _):
        for j in range(GROUP):
            where = (j % 4, lax.rem(g, 2) * 2 + j // 4, g // 2)
            parts = []
            for u in range(3):
                c1, c2, c3 = digits(where, u)
                parts.append(tb[u][c1 * 16 + c2 * 4 + c3])
            at = pl.ds(g * GS + j * SLOTS, SLOTS)
            mark = jnp.concatenate(
                [jnp.where(slot[0, at] == lane_code, one, zero), jnp.where(slot[1, at] == lane_code, one, zero)], axis=0)
            got = jnp.dot(mark, jnp.concatenate(parts, axis=0), preferred_element_type=F32).astype(BF16)
            picks[r, at] = got[:SLOTS]
            psend[at] = got[SLOTS:]
        at = pl.ds(g * GS, GS)
        small_copy(psend.at[at], picks.at[r, at], p_s.at[0], p_r.at[0], sibling).start()
        return 0

    lax.fori_loop(0, NG, take, 0)
    p_copy = small_copy(psend, picks.at[1 - r], p_s.at[0], p_r.at[0], sibling)
    p_copy.wait_recv()

    lane_slot = [(iota((256, 128), 1) + (128 * t - GS // 2)).astype(F32).astype(BF16) for t in range(GS // 128)]

    def unpack(m, _):
        at = pl.ds(m * 256, 256)
        v = vcol[at, :]
        tiles = []
        for g in range(NG):
            w = (v - (g * GS + GS // 2)).astype(BF16)
            for t in range(GS // 128):
                tiles.append(jnp.where(w == lane_slot[t], one, zero))
        mark = jnp.concatenate(tiles, axis=1)
        for h in range(2):
            cols = slice(h * 256, (h + 1) * 256)
            got = jnp.dot(mark, picks[h], preferred_element_type=F32)
            res[at, cols] = (rows[at, cols].astype(F32) - got).astype(BF16)
        return 0

    lax.fori_loop(0, ROWS // 256, unpack, 0)

    for group in (s1_copies, sc_copies, cn_copies, s2_copies, s3_copies, ag):
        for copy in group.values():
            copy.wait_send()
    for copy in (tot_copy, cx_copy, new_copy, slot_copy, p_copy):
        copy.wait_send()


def on_device(rows_in, row_codes, hot_split, codebook):
    vm = pltpu.VMEM
    dma = pltpu.SemaphoreType.DMA
    whole = pl.BlockSpec(memory_space=pltpu.VMEM)
    scratch = [
        tuple(vm((OWNERS, SLOTS, w), BF16) for w in WIDTH),
        tuple(vm((16, 4, PITCH, w), BF16) for w in WIDTH),
        vm((3, 16, 256), F32),
        tuple(vm((3, 4, KB, w), BF16) for w in WIDTH),
        tuple(vm((4, KB, w), F32) for w in WIDTH),
        tuple(vm((3, 4, KB, w), BF16) for w in WIDTH),
        tuple(vm((3, KB, w), BF16) for w in WIDTH),
        tuple(vm((KB, w), F32) for w in WIDTH),
        tuple(vm((3, KB, w), BF16) for w in WIDTH),
        tuple(vm((OWNERS, n, 256), BF16) for _, n in CUT),
        vm((8, ROWS), F32),
        vm((ROWS, 128), F32),
        vm((3, 4, 16, 128), BF16),
        vm((3, 4, 16, 128), BF16),
        vm((4, 16, 128), F32),
        vm((4, 16, 128), F32),
        vm((16, 128), F32),
        vm((3, 16, 128), F32),
        vm((16, 128), F32),
        vm((3, 16, 128), F32),
        vm((8, 128), F32),
        vm((8, 128), F32),
        vm((2, KB, 256), F32),
        vm((KB, 256), F32),
        vm((2, 64, 256), F32),
        vm((64, 256), F32),
        vm((2, OWNERS * SLOTS, 128), BF16),
        vm((2, OWNERS * SLOTS, 256), BF16),
        vm((OWNERS * SLOTS, 256), BF16),
        dma((3, 3, 4)), dma((3, 3, 4)),
        dma((3, 4)), dma((3, 4)),
        dma((3, 4)), dma((3, 4)),
        dma((3, 3, 4)), dma((3, 3, 4)),
        dma((4,)), dma((4,)),
        dma((1,)), dma((1,)),
    ]
    return pl.pallas_call(
        kernel,
        out_shape=(jax.ShapeDtypeStruct((KB // 2, E), F32), jax.ShapeDtypeStruct((ROWS, E), BF16)),
        in_specs=[whole] * 4,
        out_specs=(whole, whole),
        scratch_shapes=scratch,
        compiler_params=pltpu.CompilerParams(collective_id=0, has_side_effects=True,
                                             vmem_limit_bytes=56 * 2**20),
    )(rows_in, row_codes.reshape(LANES, 128), hot_split, codebook)


def solution(mesh):
    return jax.shard_map(
        on_device,
        mesh=mesh,
        in_specs=(P(("dp", "rep"), None), P(("dp", "rep")), P(), P("dp", None)),
        out_specs=(P(("dp", "rep"), None), P(("dp", "rep"), None)),
        check_vma=False,
    )
```

```python
import jax
import jax.numpy as jnp
from jax import lax
from jax.experimental import pallas as pl
from jax.experimental.pallas import tpu as pltpu
from jax.sharding import PartitionSpec as P

MESH = pl.DeviceIdType.MESH
F32, BF16, I32 = jnp.float32, jnp.bfloat16, jnp.int32

PRIOR = 8.0
ROWS = 2048
E = 512
KB = 128
OWNERS = 64
SLOTS = 48
PITCH = 64
GROUP = 8
GS = GROUP * SLOTS
NG = OWNERS // GROUP
LANES = ROWS // 128

WIDTH = (256, 128, 128)
COL = (0, 256, 384)
CUT = ((0, 48), (48, 48), (96, 32))

NEAR = 27
NEAR_KEPT = 24

NT = (((1,), (1,)), ((), ()))


def iota(shape, dim):
    return lax.broadcasted_iota(I32, shape, dim)


def kernel(rows_hbm, codes, hot, cb, newcb, res, rows, pk, r1, crow, s2, acc2, r2, s3, acc3, r3, tb,
           rowbuf, vcol, sc_send, sc_recv, cn1, cr1, cn2, cr2, cn3, cr3, cx, cxr,
           tot3, tot3r, nb, nbr, slot, picks, psend, held, out,
           in_s, out_s, rs_s, rs_r, sc_s, sc_r, cn_s, cn_r, ag_s, ag_r, x_s, x_r, p_s, p_r):
    d = lax.axis_index("dp")
    r = lax.axis_index("rep")
    x, y, z = lax.rem(d, 4), lax.rem(d // 4, 4), d // 16
    mine = (x, y, z)
    stride = (1, 4, 16)
    sibling = (d, 1 - r)

    def pick(seq, u, stage):
        a, b = seq[(u + stage) % 3], seq[(u + stage + 1) % 3]
        return a + r * (b - a)

    def digits(coords, u):
        return tuple(pick(coords, u, stage) for stage in range(3))

    def peer(u, stage, k):
        c = pick(mine, u, stage)
        there = lax.rem(c + k, 4)
        return (d + (there - c) * pick(stride, u, stage), r), there

    my_digits = [digits(mine, u) for u in range(3)]

    rows_copy = pltpu.make_async_copy(rows_hbm, rows, in_s)
    rows_copy.start()

    barrier = pltpu.get_barrier_semaphore()
    for axis in range(3):
        for k in range(1, 4):
            there = lax.rem(mine[axis] + k, 4)
            pl.semaphore_signal(barrier, inc=1, device_id=(d + (there - mine[axis]) * stride[axis], r),
                                device_id_type=MESH)
    pl.semaphore_signal(barrier, inc=1, device_id=sibling, device_id_type=MESH)

    def down(row):
        return jnp.transpose(jnp.broadcast_to(row, (128, 128)))

    hot_f = hot[...].astype(F32)
    hot_id = jnp.concatenate([down(hot_f[0:1, :128]), down(hot_f[0:1, 128:])], axis=0).astype(I32)
    hot_to = jnp.concatenate([down(hot_f[1:2, :128]), down(hot_f[1:2, 128:])], axis=0) + 1.0
    def order(owner):
        dx = lax.rem(owner + (4 - x), 4)
        dy = lax.rem(owner // 4 + (4 - y), 4)
        dz = lax.rem(owner // 16 + (4 - z), 4)
        ey, ez = dy - dy // 3, dz - dz // 3
        near = ez * 9 + ey * 3 + dx - dx // 3
        far = jnp.where(dz == 2, dy * 4 + dx, jnp.where(dy == 2, 16 + ez * 4 + dx, 28 + ez * 3 + ey))
        return jnp.where((dx == 2) | (dy == 2) | (dz == 2), NEAR + far, near)

    odd = lax.rem(iota((1, 128), 1), 2) == 1
    before = jnp.where(iota((128, 128), 0) < iota((128, 128), 1), 1.0, 0.0).astype(BF16)
    owner_id = iota((OWNERS, 128), 0)
    carry = jnp.zeros((OWNERS, 128), F32)
    for b in range(LANES):
        lanes = slice(b * 128, (b + 1) * 128)
        code = codes[b:b + 1, :]
        partner = jnp.sum(jnp.where(hot_id == code, hot_to, 0.0), axis=0, keepdims=True)
        code = jnp.where(odd & (partner > 0.0), partner.astype(I32) - 1, code)
        owner = code // KB
        mark = jnp.where(owner_id == owner, 1.0, 0.0)
        ahead = jnp.dot(mark.astype(BF16), before, preferred_element_type=F32) + carry
        rank = jnp.sum(mark * ahead, axis=0, keepdims=True)
        carry = carry + jnp.sum(mark, axis=1, keepdims=True)
        owner_f = owner.astype(F32)
        rowbuf[0:1, lanes] = owner_f * SLOTS + rank
        rowbuf[1:2, lanes] = owner_f
        rowbuf[2:3, lanes] = rank
        rowbuf[3:4, lanes] = (code - owner * KB).astype(F32)
        rowbuf[4:5, lanes] = order(owner).astype(F32) * SLOTS + rank

    for u in range(3):
        r1[u][:, :, :, SLOTS:, :] = jnp.zeros((4, 4, 4, PITCH - SLOTS, WIDTH[u]), BF16)

    one, zero = jnp.ones((), BF16), jnp.zeros((), BF16)
    slot_iota = (iota((GS, 128), 0) - GS // 2).astype(F32).astype(BF16)

    def slot_rows(group, kind):
        middle = (group * GS + GS // 2).astype(F32)
        tiles = []
        for b in range(LANES):
            v = jnp.broadcast_to(rowbuf[kind:kind + 1, b * 128:(b + 1) * 128] - middle, (16, 128)).astype(BF16)
            v = jnp.concatenate([v] * (GS // 16), axis=0)
            tiles.append(jnp.where(v == slot_iota, one, zero))
        return jnp.concatenate(tiles, axis=1)

    rows_copy.wait()
    pl.semaphore_wait(barrier, 10)
    def remote(src, dst, ss, rs, to):
        return pltpu.make_async_remote_copy(src, dst, ss, rs, device_id=to, device_id_type=MESH)

    s1_copies = {}
    for u in range(3):
        for k in range(1, 4):
            to, there = peer(u, 0, k)
            s1_copies[u, k] = remote(
                pk[u].at[there], r1[u].at[:, :, k, pl.ds(0, SLOTS)], rs_s.at[u, 0, k],
                rs_r.at[u, 0, k], to)

    def send_plane(oz, away, core):
        for u in range(3):
            first = (u + core) % 3
            if first == 2:
                dz = lax.rem(oz - z + 4, 4)
                src, dst = pk[u].at[oz], r1[u].at[:, :, dz, pl.ds(0, SLOTS)]

                @pl.when(away)
                def _():
                    remote(src, dst, rs_s.at[u, 0, dz], rs_r.at[u, 0, dz], (d + (oz - z) * 16, r)).start()

                @pl.when(jnp.logical_not(away))
                def _():
                    pltpu.make_async_copy(src, dst, rs_r.at[u, 0, 0]).start()
            else:
                for k in (2, 1, 3, 0):
                    to, there = peer(u, 0, k)
                    if first == 0:
                        src, dst = pk[u].at[there, :, oz], r1[u].at[:, oz, k, pl.ds(0, SLOTS)]
                    else:
                        src, dst = pk[u].at[there, oz], r1[u].at[oz, :, k, pl.ds(0, SLOTS)]
                    if k:
                        remote(src, dst, rs_s.at[u, 0, k], rs_r.at[u, 0, k], to).start()
                    else:
                        pltpu.make_async_copy(src, dst, rs_r.at[u, 0, 0]).start()

    def pack(step, _):
        oz = lax.rem(z + 2 + 3 * step, 4)
        for half in range(2):
            packed = jnp.dot(slot_rows(oz * 2 + half, 0), rows[...], preferred_element_type=F32).astype(BF16)
            for j in range(GROUP):
                where = (j % 4, half * 2 + j // 4, oz)
                for u in range(3):
                    c1, c2, c3 = digits(where, u)
                    pk[u][c1, c2, c3] = packed[j * SLOTS:(j + 1) * SLOTS, COL[u]:COL[u] + WIDTH[u]]
        for core in range(2):
            @pl.when(r == core)
            def _():
                send_plane(oz, oz != z, core)
        return 0

    lax.fori_loop(0, 4, pack, 0)

    o = rowbuf[1:2, :].astype(I32)
    coords = (lax.rem(o, 4), lax.rem(o // 4, 4), o // 16)

    def lane_tiles(f):
        return jnp.concatenate([f(slice(b * 128, (b + 1) * 128)) for b in range(LANES)], axis=1)

    id128 = iota((128, 128), 0).astype(F32)
    rank_mark = lane_tiles(lambda s: jnp.where(rowbuf[2:3, s] == id128, 1.0, 0.0).astype(BF16))
    low_mark = lane_tiles(lambda s: jnp.where(rowbuf[3:4, s] == id128, 1.0, 0.0).astype(BF16))

    sc_copies, cn_copies = {}, {}
    for u in range(3):
        c1, c2, c3 = digits(coords, u)
        place = c1 * 16 + c2 * 4 + c3
        low = lane_tiles(lambda s: jnp.where(place[:, s] == owner_id, rowbuf[3:4, s] + 1.0, 0.0).astype(BF16))
        sc = lax.dot_general(low, rank_mark, NT, preferred_element_type=F32).astype(BF16)
        for c in range(4):
            sc_send[u, c] = sc[c * 16:(c + 1) * 16]
        for k in range(1, 4):
            to, there = peer(u, 0, k)
            sc_copies[u, k] = remote(sc_send.at[u, there], sc_recv.at[u, k], sc_s.at[u, k], sc_r.at[u, k], to)
            sc_copies[u, k].start()
        if u == 0:
            own = lane_tiles(lambda s: jnp.where(place[:, s] == owner_id, 1.0, 0.0).astype(BF16))
            cn = lax.dot_general(own, low_mark, NT, preferred_element_type=F32)
            for c in range(4):
                cn1[c] = cn[c * 16:(c + 1) * 16]
            for k in range(1, 4):
                to, there = peer(0, 0, k)
                cn_copies[0, k] = remote(cn1.at[there], cr1.at[k], cn_s.at[0, k], cn_r.at[0, k], to)
                cn_copies[0, k].start()

    low_wide = lane_tiles(
        lambda s: jnp.concatenate([jnp.broadcast_to(rowbuf[3:4, s] + 1.0, (16, 128)).astype(BF16)] * 8, axis=0))

    def slot_code(g, _):
        slot[0, pl.ds(g * GS, GS)] = lax.dot_general(
            slot_rows(g, 4), low_wide, NT, preferred_element_type=F32).astype(BF16)
        return 0

    lax.fori_loop(0, NG, slot_code, 0)
    slot_copy = remote(slot.at[0], slot.at[1], x_s.at[3], x_r.at[3], sibling)
    slot_copy.start()
    for b in range(LANES):
        v = jnp.broadcast_to(rowbuf[4:5, b * 128:(b + 1) * 128], (128, 128))
        vcol[b * 128:(b + 1) * 128, :] = jnp.transpose(v)

    code_id = (iota((KB, 256), 0) + 1).astype(F32)
    s2_copies, s3_copies = {}, {}
    for u in (1, 2, 0):
        c1, c2, c3 = my_digits[u]
        pltpu.make_async_copy(pk[u].at[c1], r1[u].at[:, :, 0, pl.ds(0, SLOTS)],
                              rs_r.at[u, 0, 0]).wait()
        for k in range(1, 4):
            s1_copies[u, k].wait_recv()
            sc_copies[u, k].wait_recv()
        quarter = [sc_send[u, c1].astype(F32)] + [sc_recv[u, k].astype(F32) for k in range(1, 4)]
        crow[u, :, 0:128] = quarter[0] + pltpu.roll(quarter[1], 64, 1)
        crow[u, :, 128:256] = quarter[2] + pltpu.roll(quarter[3], 64, 1)
        for q in (1, 3, 2, 0):
            to, there = peer(u, 1, q)
            for t in range(4):
                j = there * 4 + t
                mark = jnp.where(code_id == crow[u, pl.ds(j, 1), :], 1.0, 0.0).astype(BF16)
                part = jnp.dot(mark, r1[u][there, t].reshape(4 * PITCH, WIDTH[u]), preferred_element_type=F32)
                if q == 0:
                    acc2[u][t] = part
                else:
                    s2[u][q - 1, t] = part.astype(BF16)
            if q:
                s2_copies[u, q] = remote(s2[u].at[q - 1], r2[u].at[q - 1], rs_s.at[u, 1, q], rs_r.at[u, 1, q], to)
                s2_copies[u, q].start()
        if u == 0:
            total = cn1[c1]
            for k in range(1, 4):
                cn_copies[0, k].wait_recv()
                total = total + cr1[k]
            cn2[...] = total
            for k in range(1, 4):
                cn_copies[1, k] = remote(cn2, cr2.at[k - 1], cn_s.at[1, k], cn_r.at[1, k], peer(0, 1, k)[0])
                cn_copies[1, k].start()

    for u in (1, 2, 0):
        for q in range(1, 4):
            s2_copies[u, q].wait_recv()
        for q in (1, 3, 2, 0):
            to, there = peer(u, 2, q)
            part = acc2[u][there]
            for k in range(3):
                part = part + r2[u][k, there].astype(F32)
            if q == 0:
                acc3[u][...] = part
            else:
                s3[u][q - 1] = part.astype(BF16)
                s3_copies[u, q] = remote(s3[u].at[q - 1], r3[u].at[q - 1], rs_s.at[u, 2, q], rs_r.at[u, 2, q], to)
                s3_copies[u, q].start()
        if u == 0:
            total = cn2[...]
            for k in range(1, 4):
                cn_copies[1, k].wait_recv()
                total = total + cr2[k - 1]
            cn3[...] = total
            for k in range(1, 4):
                cn_copies[2, k] = remote(cn3, cr3.at[k - 1], cn_s.at[2, k], cn_r.at[2, k], peer(0, 2, k)[0])
                cn_copies[2, k].start()

    for u in (1, 2, 0):
        part = acc3[u][...]
        for q in range(1, 4):
            s3_copies[u, q].wait_recv()
            part = part + r3[u][q - 1].astype(F32)
        if u == 0:
            tot3[0] = part
        else:
            tot3[1, :, (u - 1) * 128:u * 128] = part
    total = cn3[...]
    for k in range(1, 4):
        cn_copies[2, k].wait_recv()
        total = total + cr3[k - 1]
    mine_at = my_digits[0][1] * 4 + my_digits[0][2]
    cx[...] = jnp.broadcast_to(
        jnp.sum(jnp.where(iota((16, 128), 0) == mine_at, total, 0.0), axis=0, keepdims=True), (8, 128))
    tot_copy = remote(tot3.at[1 - r], tot3r, x_s.at[0], x_r.at[0], sibling)
    cx_copy = remote(cx, cxr, x_s.at[1], x_r.at[1], sibling)
    cx_copy.start()
    tot_copy.start()
    cx_copy.wait_recv()
    count = cx[0:1, :] + cxr[0:1, :]
    diagonal = iota((128, 128), 0) == iota((128, 128), 1)
    count = jnp.sum(jnp.where(diagonal, jnp.broadcast_to(count, (128, 128)), 0.0), axis=1, keepdims=True)
    old = jnp.where(r == 0, cb[:, :256], cb[:, 256:])
    tot_copy.wait_recv()
    new = (tot3[r] + tot3r[...] + PRIOR * old) / (count + PRIOR)
    low_new = new.astype(BF16)
    for u in range(3):
        c1, c2, c3 = my_digits[u]
        tb[u][c1, c2, c3] = low_new[CUT[u][0]:CUT[u][0] + CUT[u][1]]
    nb[0] = new[:64]
    nb[1] = new[64:]

    ag = {}

    def gather(u, stage, tag, k, block, lane):
        copy = remote(block, block, ag_s.at[u, lane], ag_r.at[u, lane], peer(u, stage, k)[0])
        copy.start()
        ag[(u,) + tag] = copy

    def line(u, e1, e2, half=None):
        c1, c2, c3 = my_digits[u]
        i1, i2 = lax.rem(c1 + e1, 4), lax.rem(c2 + e2, 4)
        return tb[u].at[i1, i2] if half is None else tb[u].at[i1, i2, pl.ds(2 * half, 2)]

    def both_ways(u, stage, tag, block, lane):
        gather(u, stage, tag + (1,), 1, block, lane)
        gather(u, stage, tag + (3,), 3, block, lane + 1)

    def pass_on(u, stage, tag, e1, e2, lane):
        step = {0: ((e1 + 3) % 4, (e1 + 1) % 4, e2, e2), 1: (e1, e1, (e2 + 3) % 4, (e2 + 1) % 4)}[stage]
        ag[(u,) + tag + (1,)].wait_recv()
        gather(u, stage, tag + ("up",), 1, line(u, step[0], step[2], 0), lane + 2)
        ag[(u,) + tag + (3,)].wait_recv()
        gather(u, stage, tag + ("down",), 3, line(u, step[1], step[3], 1), lane + 3)

    for u in range(3):
        c1, c2, c3 = my_digits[u]
        for k in range(1, 4):
            gather(u, 2, ("a", k), k, tb[u].at[c1, c2, c3], k - 1)
    new_copy = remote(nb.at[1 - r], nbr, x_s.at[2], x_r.at[2], sibling)
    new_copy.start()
    for u in range(3):
        for k in range(1, 4):
            ag[u, "a", k].wait_recv()
        both_ways(u, 1, ("b",), line(u, 0, 0), 4)
        both_ways(u, 0, ("c", 0), line(u, 0, 0), 8)
    new_copy.wait_recv()
    kept = nb[r]
    newcb[:, :256] = jnp.where(r == 0, kept, nbr[...])
    newcb[:, 256:] = jnp.where(r == 0, nbr[...], kept)
    for u in range(3):
        pass_on(u, 1, ("b",), 0, 0, 4)
        both_ways(u, 0, ("c", 1), line(u, 0, 1), 12)
        both_ways(u, 0, ("c", 3), line(u, 0, 3), 16)
    for u in range(3):
        pass_on(u, 0, ("c", 0), 0, 0, 8)
    for u in range(3):
        ag[u, "b", "up"].wait_recv()
        ag[u, "b", "down"].wait_recv()
        both_ways(u, 0, ("c", 2), line(u, 0, 2), 20)
    for u in range(3):
        pass_on(u, 0, ("c", 1), 0, 1, 12)
        pass_on(u, 0, ("c", 3), 0, 3, 16)
    slot_copy.wait_recv()

    lane_code = (iota((SLOTS, 128), 1) + 1).astype(F32).astype(BF16)

    def take(first, steps, sem):
        for j, step in enumerate(steps):
            where = tuple(lax.rem(c + e, 4) for c, e in zip(mine, step))
            parts = []
            for u in range(3):
                c1, c2, c3 = digits(where, u)
                parts.append(tb[u][c1, c2, c3])
            at = pl.ds((first + j) * SLOTS, SLOTS)
            mark = jnp.concatenate(
                [jnp.where(slot[0, at] == lane_code, one, zero), jnp.where(slot[1, at] == lane_code, one, zero)], axis=0)
            got = jnp.dot(mark, jnp.concatenate(parts, axis=0), preferred_element_type=F32).astype(BF16)
            picks[r, at] = got[:SLOTS]
            psend[at] = got[SLOTS:]
        at = pl.ds(first * SLOTS, len(steps) * SLOTS)
        remote(psend.at[at], picks.at[r, at], p_s.at[sem], p_r.at[sem], sibling).start()

    def near(ez, _):
        take(ez * 9, [((0, 1, 3)[i % 3], (0, 1, 3)[i // 3], ez + ez // 2) for i in range(9)], 0)
        return 0

    lax.fori_loop(0, 3, near, 0)
    for u in range(3):
        pass_on(u, 0, ("c", 2), 0, 2, 20)

    def slot_marks(at, begin, end):
        v = vcol[at, :]
        tiles = []
        for g in range(begin // GROUP, end // GROUP):
            w = (v - (g * GS + GS // 2)).astype(BF16)
            for t in range(GS // 128):
                tiles.append(jnp.where(w == lane_slot[t], one, zero))
        return jnp.concatenate(tiles, axis=1)

    lane_slot = [(iota((256, 128), 1) + (128 * t - GS // 2)).astype(F32).astype(BF16) for t in range(GS // 128)]
    near_rows = pl.ds(0, NEAR * SLOTS)
    far_rows = pl.ds(NEAR * SLOTS, (OWNERS - NEAR) * SLOTS)
    p_copies = [remote(psend.at[at], picks.at[1 - r, at], p_s.at[i], p_r.at[i], sibling)
                for i, at in enumerate((near_rows, far_rows))]
    p_copies[0].wait_recv()

    def unpack_near(m, _):
        at = pl.ds(m * 256, 256)
        mark = slot_marks(at, 0, NEAR_KEPT)
        for h in range(2):
            got = jnp.dot(mark, picks[h, 0:NEAR_KEPT * SLOTS], preferred_element_type=F32)
            held[h, at] = got.astype(BF16)
        return 0

    lax.fori_loop(0, ROWS // 256, unpack_near, 0)
    for u in range(3):
        for e in range(4):
            ag[u, "c", e, "up"].wait_recv()
            ag[u, "c", e, "down"].wait_recv()

    def far_z(dy, _):
        take(NEAR + dy * 4, [(i, dy, 2) for i in range(4)], 1)
        return 0

    def far_y(ez, _):
        take(NEAR + 16 + ez * 4, [(i, 2, ez + ez // 2) for i in range(4)], 1)
        return 0

    def far_x(ez, _):
        take(NEAR + 28 + ez * 3, [(2, (0, 1, 3)[i], ez + ez // 2) for i in range(3)], 1)
        return 0

    lax.fori_loop(0, 4, far_z, 0)
    lax.fori_loop(0, 3, far_y, 0)
    lax.fori_loop(0, 3, far_x, 0)

    outs = []
    for turn in range(2):
        h = r + turn * (1 - 2 * r)
        cols = pl.ds(pl.multiple_of(h * 256, 256), 256)
        if turn:
            p_copies[1].wait_recv()

        def unpack(m, _):
            at = pl.ds(m * 256, 256)
            mark = slot_marks(at, NEAR_KEPT, OWNERS)
            got = jnp.dot(mark, picks[h, NEAR_KEPT * SLOTS:], preferred_element_type=F32)
            got = got + held[h, at].astype(F32)
            out[h, at] = (rows[at, cols].astype(F32) - got).astype(BF16)
            pltpu.make_async_copy(out.at[h, at], res.at[at, cols], out_s.at[turn]).start()
            return 0

        lax.fori_loop(0, ROWS // 256, unpack, 0)
        outs.append(pltpu.make_async_copy(out.at[h], res.at[:, cols], out_s.at[turn]))
    for copy in outs:
        copy.wait()

    for group in (s1_copies, sc_copies, cn_copies, s2_copies, s3_copies, ag):
        for copy in group.values():
            copy.wait_send()
    for copy in [tot_copy, cx_copy, new_copy, slot_copy] + p_copies:
        copy.wait_send()


def hand_over(new, residual):
    parts = 4

    def copy(new_in, res_in, new_out, res_out, new_buf, res_buf, sems):
        def moves(i):
            if i == parts:
                return (pltpu.make_async_copy(new_in, new_buf, sems.at[0, i]),
                        pltpu.make_async_copy(new_buf, new_out, sems.at[1, i]))
            at = pl.ds(i * (ROWS // parts), ROWS // parts)
            return (pltpu.make_async_copy(res_in.at[at], res_buf.at[at], sems.at[0, i]),
                    pltpu.make_async_copy(res_buf.at[at], res_out.at[at], sems.at[1, i]))

        pairs = [moves(i) for i in range(parts + 1)]
        for there, _ in pairs:
            there.start()
        for there, back in pairs:
            there.wait()
            back.start()
        for _, back in pairs:
            back.wait()

    anywhere = pl.BlockSpec(memory_space=pl.ANY)
    return pl.pallas_call(
        copy,
        out_shape=(jax.ShapeDtypeStruct(new.shape, new.dtype), jax.ShapeDtypeStruct(residual.shape, residual.dtype)),
        in_specs=[anywhere] * 2,
        out_specs=(anywhere, anywhere),
        scratch_shapes=[pltpu.VMEM(new.shape, new.dtype), pltpu.VMEM(residual.shape, residual.dtype),
                        pltpu.SemaphoreType.DMA((2, parts + 1))],
    )(new, residual)


def on_device(rows_in, row_codes, hot_split, codebook):
    vm = pltpu.VMEM
    dma = pltpu.SemaphoreType.DMA
    whole = pl.BlockSpec(memory_space=pltpu.VMEM)
    scratch = [
        vm((ROWS, E), BF16),
        tuple(vm((4, 4, 4, SLOTS, w), BF16) for w in WIDTH),
        tuple(vm((4, 4, 4, PITCH, w), BF16) for w in WIDTH),
        vm((3, 16, 256), F32),
        tuple(vm((3, 4, KB, w), BF16) for w in WIDTH),
        tuple(vm((4, KB, w), F32) for w in WIDTH),
        tuple(vm((3, 4, KB, w), BF16) for w in WIDTH),
        tuple(vm((3, KB, w), BF16) for w in WIDTH),
        tuple(vm((KB, w), F32) for w in WIDTH),
        tuple(vm((3, KB, w), BF16) for w in WIDTH),
        tuple(vm((4, 4, 4, n, 256), BF16) for _, n in CUT),
        vm((8, ROWS), F32),
        vm((ROWS, 128), F32),
        vm((3, 4, 16, 128), BF16),
        vm((3, 4, 16, 128), BF16),
        vm((4, 16, 128), F32),
        vm((4, 16, 128), F32),
        vm((16, 128), F32),
        vm((3, 16, 128), F32),
        vm((16, 128), F32),
        vm((3, 16, 128), F32),
        vm((8, 128), F32),
        vm((8, 128), F32),
        vm((2, KB, 256), F32),
        vm((KB, 256), F32),
        vm((2, 64, 256), F32),
        vm((64, 256), F32),
        vm((2, OWNERS * SLOTS, 128), BF16),
        vm((2, OWNERS * SLOTS, 256), BF16),
        vm((OWNERS * SLOTS, 256), BF16),
        vm((2, ROWS, 256), BF16),
        vm((2, ROWS, 256), BF16),
        dma, dma((2,)),
        dma((3, 3, 4)), dma((3, 3, 4)),
        dma((3, 4)), dma((3, 4)),
        dma((3, 4)), dma((3, 4)),
        dma((3, 24)), dma((3, 24)),
        dma((4,)), dma((4,)),
        dma((2,)), dma((2,)),
    ]
    new, residual = pl.pallas_call(
        kernel,
        out_shape=(jax.ShapeDtypeStruct((KB // 2, E), F32), jax.ShapeDtypeStruct((ROWS, E), BF16)),
        in_specs=[pl.BlockSpec(memory_space=pl.ANY)] + [whole] * 3,
        out_specs=(whole, pl.BlockSpec(memory_space=pl.ANY)),
        scratch_shapes=scratch,
        compiler_params=pltpu.CompilerParams(collective_id=0, has_side_effects=True,
                                             vmem_limit_bytes=56 * 2**20),
    )(rows_in, row_codes.reshape(LANES, 128), hot_split.T, codebook)
    return hand_over(new, residual)


def solution(mesh):
    return jax.shard_map(
        on_device,
        mesh=mesh,
        in_specs=(P(("dp", "rep"), None), P(("dp", "rep")), P(), P("dp", None)),
        out_specs=(P(("dp", "rep"), None), P(("dp", "rep"), None)),
        check_vma=False,
    )
```

```python
import jax
import jax.numpy as jnp
from jax import lax
from jax.experimental import pallas as pl
from jax.experimental.pallas import tpu as pltpu
from jax.sharding import PartitionSpec as P

MESH = pl.DeviceIdType.MESH
F32, BF16, I32 = jnp.float32, jnp.bfloat16, jnp.int32

PRIOR = 8.0
ROWS = 2048
E = 512
KB = 128
OWNERS = 64
SLOTS = 48
PITCH = 64
GROUP = 8
GS = GROUP * SLOTS
NG = OWNERS // GROUP
LANES = ROWS // 128

WIDTH = (256, 128, 128)
COL = (0, 256, 384)
CUT = ((0, 48), (48, 48), (96, 32))

NEAR = 27
NEAR_KEPT = 24

NT = (((1,), (1,)), ((), ()))


def iota(shape, dim):
    return lax.broadcasted_iota(I32, shape, dim)


def kernel(rows_hbm, codes_hbm, hot_hbm, cb_hbm, newcb, res, rows, codes, hot, old, new_out, pk, r1, crow, s2, t2, own2, r2, s3, acc3, r3, tb,
           rowbuf, vcol, sc_send, sc_recv, cn1, cr1, cn2, cr2, cn3, cr3, cx, cxr,
           tot3, tot3r, nb, nbr, slot, picks, psend, held, out,
           in_s, out_s, w_s, w_r, rs_s, rs_r, sc_s, sc_r, cn_s, cn_r, ag_s, ag_r, x_s, x_r, p_s, p_r):
    d = lax.axis_index("dp")
    r = lax.axis_index("rep")
    x, y, z = lax.rem(d, 4), lax.rem(d // 4, 4), d // 16
    mine = (x, y, z)
    stride = (1, 4, 16)
    sibling = (d, 1 - r)

    def pick(seq, u, stage):
        a, b = seq[(u + stage) % 3], seq[(u + stage + 1) % 3]
        return a + r * (b - a)

    def digits(coords, u):
        return tuple(pick(coords, u, stage) for stage in range(3))

    def peer(u, stage, k):
        c = pick(mine, u, stage)
        there = lax.rem(c + k, 4)
        return (d + (there - c) * pick(stride, u, stage), r), there

    my_digits = [digits(mine, u) for u in range(3)]

    barrier = pltpu.get_barrier_semaphore()
    for axis in range(3):
        for k in range(1, 4):
            there = lax.rem(mine[axis] + k, 4)
            pl.semaphore_signal(barrier, inc=1, device_id=(d + (there - mine[axis]) * stride[axis], r),
                                device_id_type=MESH)
    pl.semaphore_signal(barrier, inc=1, device_id=sibling, device_id_type=MESH)

    codes_copy = pltpu.make_async_copy(codes_hbm, codes, in_s.at[0])
    hot_copy = pltpu.make_async_copy(hot_hbm, hot, in_s.at[1])
    rows_copy = pltpu.make_async_copy(rows_hbm, rows, in_s.at[2])
    old_copy = pltpu.make_async_copy(cb_hbm.at[:, pl.ds(pl.multiple_of(r * 256, 256), 256)], old, in_s.at[3])
    for copy in (codes_copy, hot_copy, rows_copy, old_copy):
        copy.start()
    hot_copy.wait()
    codes_copy.wait()

    def down(row):
        return jnp.transpose(jnp.broadcast_to(row, (128, 128)))

    hot_f = hot[...].astype(F32)
    hot_id = jnp.concatenate([down(hot_f[0:1, :128]), down(hot_f[0:1, 128:])], axis=0).astype(I32)
    hot_to = jnp.concatenate([down(hot_f[1:2, :128]), down(hot_f[1:2, 128:])], axis=0) + 1.0
    def order(owner):
        dx = lax.rem(owner + (4 - x), 4)
        dy = lax.rem(owner // 4 + (4 - y), 4)
        dz = lax.rem(owner // 16 + (4 - z), 4)
        ey, ez = dy - dy // 3, dz - dz // 3
        near = ez * 9 + ey * 3 + dx - dx // 3
        far = jnp.where(dz == 2, dy * 4 + dx, jnp.where(dy == 2, 16 + ez * 4 + dx, 28 + ez * 3 + ey))
        return jnp.where((dx == 2) | (dy == 2) | (dz == 2), NEAR + far, near)

    odd = lax.rem(iota((1, 128), 1), 2) == 1
    before = jnp.where(iota((128, 128), 0) < iota((128, 128), 1), 1.0, 0.0).astype(BF16)
    owner_id = iota((OWNERS, 128), 0)
    carry = jnp.zeros((OWNERS, 128), F32)
    for b in range(LANES):
        lanes = slice(b * 128, (b + 1) * 128)
        code = codes[b:b + 1, :]
        partner = jnp.sum(jnp.where(hot_id == code, hot_to, 0.0), axis=0, keepdims=True)
        code = jnp.where(odd & (partner > 0.0), partner.astype(I32) - 1, code)
        owner = code // KB
        mark = jnp.where(owner_id == owner, 1.0, 0.0)
        ahead = jnp.dot(mark.astype(BF16), before, preferred_element_type=F32) + carry
        rank = jnp.sum(mark * ahead, axis=0, keepdims=True)
        carry = carry + jnp.sum(mark, axis=1, keepdims=True)
        owner_f = owner.astype(F32)
        rowbuf[0:1, lanes] = owner_f * SLOTS + rank
        rowbuf[1:2, lanes] = owner_f
        rowbuf[2:3, lanes] = rank
        rowbuf[3:4, lanes] = (code - owner * KB).astype(F32)
        rowbuf[4:5, lanes] = order(owner).astype(F32) * SLOTS + rank

    for u in range(3):
        r1[u][:, :, :, SLOTS:, :] = jnp.zeros((4, 4, 4, PITCH - SLOTS, WIDTH[u]), BF16)

    one, zero = jnp.ones((), BF16), jnp.zeros((), BF16)
    slot_iota = (iota((GS, 128), 0) - GS // 2).astype(F32).astype(BF16)

    def slot_rows(group, kind):
        middle = (group * GS + GS // 2).astype(F32)
        tiles = []
        for b in range(LANES):
            v = jnp.broadcast_to(rowbuf[kind:kind + 1, b * 128:(b + 1) * 128] - middle, (16, 128)).astype(BF16)
            v = jnp.concatenate([v] * (GS // 16), axis=0)
            tiles.append(jnp.where(v == slot_iota, one, zero))
        return jnp.concatenate(tiles, axis=1)

    rows_copy.wait()
    pl.semaphore_wait(barrier, 10)
    def remote(src, dst, ss, rs, to):
        return pltpu.make_async_remote_copy(src, dst, ss, rs, device_id=to, device_id_type=MESH)

    s1_copies = {}
    for u in range(3):
        for k in range(1, 4):
            to, there = peer(u, 0, k)
            s1_copies[u, k] = remote(
                pk[u].at[there], r1[u].at[:, :, k, pl.ds(0, SLOTS)], rs_s.at[u, 0, k],
                rs_r.at[u, 0, k], to)

    def send_plane(oz, away, core):
        for u in range(3):
            first = (u + core) % 3
            if first == 2:
                dz = lax.rem(oz - z + 4, 4)
                src, dst = pk[u].at[oz], r1[u].at[:, :, dz, pl.ds(0, SLOTS)]

                @pl.when(away)
                def _():
                    remote(src, dst, rs_s.at[u, 0, dz], rs_r.at[u, 0, dz], (d + (oz - z) * 16, r)).start()

                @pl.when(jnp.logical_not(away))
                def _():
                    pltpu.make_async_copy(src, dst, rs_r.at[u, 0, 0]).start()
            else:
                for k in (2, 1, 3, 0):
                    to, there = peer(u, 0, k)
                    if first == 0:
                        src, dst = pk[u].at[there, :, oz], r1[u].at[:, oz, k, pl.ds(0, SLOTS)]
                    else:
                        src, dst = pk[u].at[there, oz], r1[u].at[oz, :, k, pl.ds(0, SLOTS)]
                    if k:
                        remote(src, dst, rs_s.at[u, 0, k], rs_r.at[u, 0, k], to).start()
                    else:
                        pltpu.make_async_copy(src, dst, rs_r.at[u, 0, 0]).start()

    def pack(step, _):
        oz = lax.rem(z + 2 + 3 * step, 4)
        for half in range(2):
            packed = jnp.dot(slot_rows(oz * 2 + half, 0), rows[...], preferred_element_type=F32).astype(BF16)
            for j in range(GROUP):
                where = (j % 4, half * 2 + j // 4, oz)
                for u in range(3):
                    c1, c2, c3 = digits(where, u)
                    pk[u][c1, c2, c3] = packed[j * SLOTS:(j + 1) * SLOTS, COL[u]:COL[u] + WIDTH[u]]
        for core in range(2):
            @pl.when(r == core)
            def _():
                send_plane(oz, oz != z, core)
        return 0

    lax.fori_loop(0, 4, pack, 0)

    o = rowbuf[1:2, :].astype(I32)
    coords = (lax.rem(o, 4), lax.rem(o // 4, 4), o // 16)

    def lane_tiles(f):
        return jnp.concatenate([f(slice(b * 128, (b + 1) * 128)) for b in range(LANES)], axis=1)

    id128 = iota((128, 128), 0).astype(F32)
    rank_mark = lane_tiles(lambda s: jnp.where(rowbuf[2:3, s] == id128, 1.0, 0.0).astype(BF16))
    low_mark = lane_tiles(lambda s: jnp.where(rowbuf[3:4, s] == id128, 1.0, 0.0).astype(BF16))

    sc_copies, cn_copies = {}, {}
    for u in range(3):
        c1, c2, c3 = digits(coords, u)
        place = c1 * 16 + c2 * 4 + c3
        low = lane_tiles(lambda s: jnp.where(place[:, s] == owner_id, rowbuf[3:4, s] + 1.0, 0.0).astype(BF16))
        sc = lax.dot_general(low, rank_mark, NT, preferred_element_type=F32).astype(BF16)
        for c in range(4):
            sc_send[u, c] = sc[c * 16:(c + 1) * 16]
        for k in range(1, 4):
            to, there = peer(u, 0, k)
            sc_copies[u, k] = remote(sc_send.at[u, there], sc_recv.at[u, k], sc_s.at[u, k], sc_r.at[u, k], to)
            sc_copies[u, k].start()
        if u == 0:
            own = lane_tiles(lambda s: jnp.where(place[:, s] == owner_id, 1.0, 0.0).astype(BF16))
            cn = lax.dot_general(own, low_mark, NT, preferred_element_type=F32)
            for c in range(4):
                cn1[c] = cn[c * 16:(c + 1) * 16]
            for k in range(1, 4):
                to, there = peer(0, 0, k)
                cn_copies[0, k] = remote(cn1.at[there], cr1.at[k], cn_s.at[0, k], cn_r.at[0, k], to)
                cn_copies[0, k].start()

    low_wide = lane_tiles(
        lambda s: jnp.concatenate([jnp.broadcast_to(rowbuf[3:4, s] + 1.0, (16, 128)).astype(BF16)] * 8, axis=0))

    def slot_code(g, _):
        slot[0, pl.ds(g * GS, GS)] = lax.dot_general(
            slot_rows(g, 4), low_wide, NT, preferred_element_type=F32).astype(BF16)
        return 0

    lax.fori_loop(0, NG, slot_code, 0)
    slot_copy = remote(slot.at[0], slot.at[1], x_s.at[3], x_r.at[3], sibling)
    slot_copy.start()
    for b in range(LANES):
        v = jnp.broadcast_to(rowbuf[4:5, b * 128:(b + 1) * 128], (128, 128))
        vcol[b * 128:(b + 1) * 128, :] = jnp.transpose(v)

    code_id = (iota((KB, 256), 0) + 1).astype(F32)
    s2_copies, s3_copies = {}, {}
    def ring_sum(u, q, t):
        there = peer(u, 1, q)[1]
        mark = jnp.where(code_id == crow[u, pl.ds(there * 4 + t, 1), :], 1.0, 0.0).astype(BF16)
        return jnp.dot(mark, r1[u][there, t].reshape(4 * PITCH, WIDTH[u]), preferred_element_type=F32)

    def send_sum(u, name, src, dst, lane, k):
        s2_copies[(u,) + name] = remote(src, dst, w_s.at[u, lane], w_r.at[u, lane], peer(u, 1, k)[0])
        s2_copies[(u,) + name].start()

    halves = (pl.ds(0, 2), pl.ds(2, 2))
    for u in (1, 2, 0):
        c1, c2, c3 = my_digits[u]
        pltpu.make_async_copy(pk[u].at[c1], r1[u].at[:, :, 0, pl.ds(0, SLOTS)],
                              rs_r.at[u, 0, 0]).wait()
        for k in range(1, 4):
            s1_copies[u, k].wait_recv()
            sc_copies[u, k].wait_recv()
        quarter = [sc_send[u, c1].astype(F32)] + [sc_recv[u, k].astype(F32) for k in range(1, 4)]
        crow[u, :, 0:128] = quarter[0] + pltpu.roll(quarter[1], 64, 1)
        crow[u, :, 128:256] = quarter[2] + pltpu.roll(quarter[3], 64, 1)
        parts = [ring_sum(u, 2, t).astype(BF16) for t in range(4)]
        for t in range(4):
            s2[u][1, t] = parts[t]
        for half in range(2):
            send_sum(u, ("via", half), s2[u].at[1, halves[half]], t2[u].at[half], half, (1, 3)[half])
    for u in (1, 2, 0):
        order2 = ((1, 2), (1, 3), (3, 0), (3, 1))
        parts = [ring_sum(u, q, t).astype(BF16) for q, t in order2]
        for (q, t), part in zip(order2, parts):
            s2[u][q - 1, t] = part
        for half, q in ((1, 1), (0, 3)):
            send_sum(u, ("whole", q), s2[u].at[q - 1, halves[half]], r2[u].at[q // 2, halves[half]], 2 + q // 2, q)
    u, c1 = 0, my_digits[0][0]
    total = cn1[c1]
    for k in range(1, 4):
        cn_copies[0, k].wait_recv()
        total = total + cr1[k]
    cn2[...] = total
    for k in range(1, 4):
        cn_copies[1, k] = remote(cn2, cr2.at[k - 1], cn_s.at[1, k], cn_r.at[1, k], peer(0, 1, k)[0])
        cn_copies[1, k].start()

    for u in (1, 2, 0):
        for half, q in ((0, 1), (1, 3)):
            parts = [ring_sum(u, q, 2 * half + t) for t in range(2)]
            s2_copies[u, "via", half].wait_recv()
            for t in range(2):
                s2[u][q - 1, 2 * half + t] = (parts[t] + t2[u][half, t].astype(F32)).astype(BF16)
            send_sum(u, ("added", q), s2[u].at[q - 1, halves[half]], r2[u].at[q // 2, halves[half]], 4 + q // 2, q)
    for u in (1, 2, 0):
        for t in range(4):
            own2[u][t] = ring_sum(u, 0, t)

    for u in (1, 2, 0):
        for name in ("whole", "added"):
            for q in (1, 3):
                s2_copies[u, name, q].wait_recv()
        for q in (1, 3, 2, 0):
            to, there = peer(u, 2, q)
            part = own2[u][there]
            for k in range(2):
                part = part + r2[u][k, there].astype(F32)
            if q == 0:
                acc3[u][...] = part
            else:
                s3[u][q - 1] = part.astype(BF16)
                s3_copies[u, q] = remote(s3[u].at[q - 1], r3[u].at[q - 1], rs_s.at[u, 2, q], rs_r.at[u, 2, q], to)
                s3_copies[u, q].start()
        if u == 0:
            total = cn2[...]
            for k in range(1, 4):
                cn_copies[1, k].wait_recv()
                total = total + cr2[k - 1]
            cn3[...] = total
            for k in range(1, 4):
                cn_copies[2, k] = remote(cn3, cr3.at[k - 1], cn_s.at[2, k], cn_r.at[2, k], peer(0, 2, k)[0])
                cn_copies[2, k].start()

    for u in (1, 2, 0):
        part = acc3[u][...]
        for q in range(1, 4):
            s3_copies[u, q].wait_recv()
            part = part + r3[u][q - 1].astype(F32)
        if u == 0:
            tot3[0] = part
        else:
            tot3[1, :, (u - 1) * 128:u * 128] = part
    total = cn3[...]
    for k in range(1, 4):
        cn_copies[2, k].wait_recv()
        total = total + cr3[k - 1]
    mine_at = my_digits[0][1] * 4 + my_digits[0][2]
    cx[...] = jnp.broadcast_to(
        jnp.sum(jnp.where(iota((16, 128), 0) == mine_at, total, 0.0), axis=0, keepdims=True), (8, 128))
    tot_copy = remote(tot3.at[1 - r], tot3r, x_s.at[0], x_r.at[0], sibling)
    cx_copy = remote(cx, cxr, x_s.at[1], x_r.at[1], sibling)
    cx_copy.start()
    tot_copy.start()
    cx_copy.wait_recv()
    count = cx[0:1, :] + cxr[0:1, :]
    diagonal = iota((128, 128), 0) == iota((128, 128), 1)
    count = jnp.sum(jnp.where(diagonal, jnp.broadcast_to(count, (128, 128)), 0.0), axis=1, keepdims=True)
    old_copy.wait()
    tot_copy.wait_recv()
    new = (tot3[r] + tot3r[...] + PRIOR * old[...]) / (count + PRIOR)
    low_new = new.astype(BF16)
    for u in range(3):
        c1, c2, c3 = my_digits[u]
        tb[u][c1, c2, c3] = low_new[CUT[u][0]:CUT[u][0] + CUT[u][1]]
    nb[0] = new[:64]
    nb[1] = new[64:]

    ag = {}

    def gather(u, stage, tag, k, block, lane):
        copy = remote(block, block, ag_s.at[u, lane], ag_r.at[u, lane], peer(u, stage, k)[0])
        copy.start()
        ag[(u,) + tag] = copy

    def line(u, e1, e2, half=None):
        c1, c2, c3 = my_digits[u]
        i1, i2 = lax.rem(c1 + e1, 4), lax.rem(c2 + e2, 4)
        return tb[u].at[i1, i2] if half is None else tb[u].at[i1, i2, pl.ds(2 * half, 2)]

    def both_ways(u, stage, tag, block, lane):
        gather(u, stage, tag + (1,), 1, block, lane)
        gather(u, stage, tag + (3,), 3, block, lane + 1)

    def pass_on(u, stage, tag, e1, e2, lane):
        step = {0: ((e1 + 3) % 4, (e1 + 1) % 4, e2, e2), 1: (e1, e1, (e2 + 3) % 4, (e2 + 1) % 4)}[stage]
        ag[(u,) + tag + (1,)].wait_recv()
        gather(u, stage, tag + ("up",), 1, line(u, step[0], step[2], 0), lane + 2)
        ag[(u,) + tag + (3,)].wait_recv()
        gather(u, stage, tag + ("down",), 3, line(u, step[1], step[3], 1), lane + 3)

    for u in range(3):
        c1, c2, c3 = my_digits[u]
        for k in range(1, 4):
            gather(u, 2, ("a", k), k, tb[u].at[c1, c2, c3], k - 1)
    new_copy = remote(nb.at[1 - r], nbr, x_s.at[2], x_r.at[2], sibling)
    new_copy.start()
    for u in range(3):
        for k in range(1, 4):
            ag[u, "a", k].wait_recv()
        both_ways(u, 1, ("b",), line(u, 0, 0), 4)
        both_ways(u, 0, ("c", 0), line(u, 0, 0), 8)
    new_copy.wait_recv()
    kept = nb[r]
    new_out[:, :256] = jnp.where(r == 0, kept, nbr[...])
    new_out[:, 256:] = jnp.where(r == 0, nbr[...], kept)
    new_out_copy = pltpu.make_async_copy(new_out, newcb, out_s.at[2])
    new_out_copy.start()
    for u in range(3):
        pass_on(u, 1, ("b",), 0, 0, 4)
        both_ways(u, 0, ("c", 1), line(u, 0, 1), 12)
        both_ways(u, 0, ("c", 3), line(u, 0, 3), 16)
    for u in range(3):
        pass_on(u, 0, ("c", 0), 0, 0, 8)
    for u in range(3):
        ag[u, "b", "up"].wait_recv()
        ag[u, "b", "down"].wait_recv()
        both_ways(u, 0, ("c", 2), line(u, 0, 2), 20)
    for u in range(3):
        pass_on(u, 0, ("c", 1), 0, 1, 12)
        pass_on(u, 0, ("c", 3), 0, 3, 16)
    slot_copy.wait_recv()

    lane_code = (iota((SLOTS, 128), 1) + 1).astype(F32).astype(BF16)

    def take(first, steps, sem):
        for begin in range(0, len(steps), 3):
            found = []
            for j in range(begin, min(begin + 3, len(steps))):
                where = tuple(lax.rem(c + e, 4) for c, e in zip(mine, steps[j]))
                parts = []
                for u in range(3):
                    c1, c2, c3 = digits(where, u)
                    parts.append(tb[u][c1, c2, c3])
                at = pl.ds((first + j) * SLOTS, SLOTS)
                mark = jnp.concatenate([jnp.where(slot[i, at] == lane_code, one, zero) for i in range(2)], axis=0)
                got = jnp.dot(mark, jnp.concatenate(parts, axis=0), preferred_element_type=F32)
                found.append((at, got.astype(BF16)))
            for at, got in found:
                picks[r, at] = got[:SLOTS]
                psend[at] = got[SLOTS:]
        at = pl.ds(first * SLOTS, len(steps) * SLOTS)
        remote(psend.at[at], picks.at[r, at], p_s.at[sem], p_r.at[sem], sibling).start()

    def near(ez, _):
        take(ez * 9, [((0, 1, 3)[i % 3], (0, 1, 3)[i // 3], ez + ez // 2) for i in range(9)], 0)
        return 0

    lax.fori_loop(0, 3, near, 0)
    for u in range(3):
        pass_on(u, 0, ("c", 2), 0, 2, 20)

    def slot_marks(at, begin, end):
        v = vcol[at, :]
        tiles = []
        for g in range(begin // GROUP, end // GROUP):
            w = (v - (g * GS + GS // 2)).astype(BF16)
            for t in range(GS // 128):
                tiles.append(jnp.where(w == lane_slot[t], one, zero))
        return jnp.concatenate(tiles, axis=1)

    lane_slot = [(iota((256, 128), 1) + (128 * t - GS // 2)).astype(F32).astype(BF16) for t in range(GS // 128)]
    near_rows = pl.ds(0, NEAR * SLOTS)
    far_rows = pl.ds(NEAR * SLOTS, (OWNERS - NEAR) * SLOTS)
    p_copies = [remote(psend.at[at], picks.at[1 - r, at], p_s.at[i], p_r.at[i], sibling)
                for i, at in enumerate((near_rows, far_rows))]
    p_copies[0].wait_recv()

    def unpack_near(m, _):
        at = pl.ds(m * 256, 256)
        mark = slot_marks(at, 0, NEAR_KEPT)
        for h in range(2):
            got = jnp.dot(mark, picks[h, 0:NEAR_KEPT * SLOTS], preferred_element_type=F32)
            held[h, at] = got.astype(BF16)
        return 0

    lax.fori_loop(0, ROWS // 256, unpack_near, 0)
    for u in range(3):
        for e in range(4):
            ag[u, "c", e, "up"].wait_recv()
            ag[u, "c", e, "down"].wait_recv()

    def far_z(dy, _):
        take(NEAR + dy * 4, [(i, dy, 2) for i in range(4)], 1)
        return 0

    def far_y(ez, _):
        take(NEAR + 16 + ez * 4, [(i, 2, ez + ez // 2) for i in range(4)], 1)
        return 0

    def far_x(ez, _):
        take(NEAR + 28 + ez * 3, [(2, (0, 1, 3)[i], ez + ez // 2) for i in range(3)], 1)
        return 0

    lax.fori_loop(0, 4, far_z, 0)
    lax.fori_loop(0, 3, far_y, 0)
    lax.fori_loop(0, 3, far_x, 0)

    outs = []
    for turn in range(2):
        h = r + turn * (1 - 2 * r)
        cols = pl.ds(pl.multiple_of(h * 256, 256), 256)
        if turn:
            p_copies[1].wait_recv()

        def unpack(m, _):
            at = pl.ds(m * 256, 256)
            mark = slot_marks(at, NEAR_KEPT, OWNERS)
            got = jnp.dot(mark, picks[h, NEAR_KEPT * SLOTS:], preferred_element_type=F32)
            got = got + held[h, at].astype(F32)
            out[h, at] = (rows[at, cols].astype(F32) - got).astype(BF16)
            pltpu.make_async_copy(out.at[h, at], res.at[at, cols], out_s.at[turn]).start()
            return 0

        lax.fori_loop(0, ROWS // 256, unpack, 0)
        outs.append(pltpu.make_async_copy(out.at[h], res.at[:, cols], out_s.at[turn]))
    new_out_copy.wait()
    for copy in outs:
        copy.wait()

    for group in (s1_copies, sc_copies, cn_copies, s2_copies, s3_copies, ag):
        for copy in group.values():
            copy.wait_send()
    for copy in [tot_copy, cx_copy, new_copy, slot_copy] + p_copies:
        copy.wait_send()


def hand_over(new, residual):
    parts = 4

    def copy(new_in, res_in, new_out, res_out, new_buf, res_buf, sems):
        def moves(i):
            if i == parts:
                return (pltpu.make_async_copy(new_in, new_buf, sems.at[0, i]),
                        pltpu.make_async_copy(new_buf, new_out, sems.at[1, i]))
            at = pl.ds(i * (ROWS // parts), ROWS // parts)
            return (pltpu.make_async_copy(res_in.at[at], res_buf.at[at], sems.at[0, i]),
                    pltpu.make_async_copy(res_buf.at[at], res_out.at[at], sems.at[1, i]))

        pairs = [moves(i) for i in range(parts + 1)]
        for there, _ in pairs:
            there.start()
        for there, back in pairs:
            there.wait()
            back.start()
        for _, back in pairs:
            back.wait()

    anywhere = pl.BlockSpec(memory_space=pl.ANY)
    return pl.pallas_call(
        copy,
        out_shape=(jax.ShapeDtypeStruct(new.shape, new.dtype), jax.ShapeDtypeStruct(residual.shape, residual.dtype)),
        in_specs=[anywhere] * 2,
        out_specs=(anywhere, anywhere),
        scratch_shapes=[pltpu.VMEM(new.shape, new.dtype), pltpu.VMEM(residual.shape, residual.dtype),
                        pltpu.SemaphoreType.DMA((2, parts + 1))],
    )(new, residual)


def on_device(rows_in, row_codes, hot_split, codebook):
    vm = pltpu.VMEM
    dma = pltpu.SemaphoreType.DMA
    anywhere = pl.BlockSpec(memory_space=pl.ANY)
    scratch = [
        vm((ROWS, E), BF16),
        vm((LANES, 128), I32),
        vm((2, 256), I32),
        vm((KB, 256), F32),
        vm((KB // 2, E), F32),
        tuple(vm((4, 4, 4, SLOTS, w), BF16) for w in WIDTH),
        tuple(vm((4, 4, 4, PITCH, w), BF16) for w in WIDTH),
        vm((3, 16, 256), F32),
        tuple(vm((3, 4, KB, w), BF16) for w in WIDTH),
        tuple(vm((2, 2, KB, w), BF16) for w in WIDTH),
        tuple(vm((4, KB, w), F32) for w in WIDTH),
        tuple(vm((2, 4, KB, w), BF16) for w in WIDTH),
        tuple(vm((3, KB, w), BF16) for w in WIDTH),
        tuple(vm((KB, w), F32) for w in WIDTH),
        tuple(vm((3, KB, w), BF16) for w in WIDTH),
        tuple(vm((4, 4, 4, n, 256), BF16) for _, n in CUT),
        vm((8, ROWS), F32),
        vm((ROWS, 128), F32),
        vm((3, 4, 16, 128), BF16),
        vm((3, 4, 16, 128), BF16),
        vm((4, 16, 128), F32),
        vm((4, 16, 128), F32),
        vm((16, 128), F32),
        vm((3, 16, 128), F32),
        vm((16, 128), F32),
        vm((3, 16, 128), F32),
        vm((8, 128), F32),
        vm((8, 128), F32),
        vm((2, KB, 256), F32),
        vm((KB, 256), F32),
        vm((2, 64, 256), F32),
        vm((64, 256), F32),
        vm((2, OWNERS * SLOTS, 128), BF16),
        vm((2, OWNERS * SLOTS, 256), BF16),
        vm((OWNERS * SLOTS, 256), BF16),
        vm((2, ROWS, 256), BF16),
        vm((2, ROWS, 256), BF16),
        dma((4,)), dma((3,)),
        dma((3, 6)), dma((3, 6)),
        dma((3, 3, 4)), dma((3, 3, 4)),
        dma((3, 4)), dma((3, 4)),
        dma((3, 4)), dma((3, 4)),
        dma((3, 24)), dma((3, 24)),
        dma((4,)), dma((4,)),
        dma((2,)), dma((2,)),
    ]
    new, residual = pl.pallas_call(
        kernel,
        out_shape=(jax.ShapeDtypeStruct((KB // 2, E), F32), jax.ShapeDtypeStruct((ROWS, E), BF16)),
        in_specs=[anywhere] * 4,
        out_specs=(anywhere, anywhere),
        scratch_shapes=scratch,
        compiler_params=pltpu.CompilerParams(collective_id=0, has_side_effects=True,
                                             vmem_limit_bytes=56 * 2**20),
    )(rows_in, row_codes.reshape(LANES, 128), hot_split.T, codebook)
    return hand_over(new, residual)


def solution(mesh):
    return jax.shard_map(
        on_device,
        mesh=mesh,
        in_specs=(P(("dp", "rep"), None), P(("dp", "rep")), P(), P("dp", None)),
        out_specs=(P(("dp", "rep"), None), P(("dp", "rep"), None)),
        check_vma=False,
    )
```

```python
import jax
import jax.numpy as jnp
from jax import lax
from jax.experimental import pallas as pl
from jax.experimental.pallas import tpu as pltpu
from jax.sharding import PartitionSpec as P

MESH = pl.DeviceIdType.MESH
F32, BF16, I32 = jnp.float32, jnp.bfloat16, jnp.int32

PRIOR = 8.0
ROWS = 2048
E = 512
KB = 128
BLOCK = 1024
OWNERS = 64
SLOTS = 48
PITCH = 64
GROUP = 8
GS = GROUP * SLOTS
NG = OWNERS // GROUP
LANES = ROWS // 128

WIDTH = (256, 128, 128)
COL = (0, 256, 384)
CUT = ((0, 48), (48, 48), (96, 32))

NEAR = 27
NEAR_KEPT = 24

NT = (((1,), (1,)), ((), ()))


def iota(shape, dim):
    return lax.broadcasted_iota(I32, shape, dim)


def kernel(rows_hbm, codes_hbm, hot_hbm, cb_hbm, newcb, res, rows, codes, hot, old, new_out, pk, r1, crow, s2, t2, own2, r2, s3, acc3, r3, tb,
           split, rowbuf, vcol, sc_send, sc_recv, cn1, cr1, cn2, cr2, cn3, cr3, cx, cxr,
           tot3, tot3r, nb, nbr, slot, picks, psend, held, out,
           in_s, out_s, w_s, w_r, rs_s, rs_r, sc_s, sc_r, cn_s, cn_r, ag_s, ag_r, x_s, x_r, p_s, p_r):
    d = lax.axis_index("dp")
    r = lax.axis_index("rep")
    x, y, z = lax.rem(d, 4), lax.rem(d // 4, 4), d // 16
    mine = (x, y, z)
    stride = (1, 4, 16)
    sibling = (d, 1 - r)

    def pick(seq, u, stage):
        a, b = seq[(u + stage) % 3], seq[(u + stage + 1) % 3]
        return a + r * (b - a)

    def digits(coords, u):
        return tuple(pick(coords, u, stage) for stage in range(3))

    def peer(u, stage, k):
        c = pick(mine, u, stage)
        there = lax.rem(c + k, 4)
        return (d + (there - c) * pick(stride, u, stage), r), there

    my_digits = [digits(mine, u) for u in range(3)]

    barrier = pltpu.get_barrier_semaphore()
    for axis in range(3):
        for k in range(1, 4):
            there = lax.rem(mine[axis] + k, 4)
            pl.semaphore_signal(barrier, inc=1, device_id=(d + (there - mine[axis]) * stride[axis], r),
                                device_id_type=MESH)
    pl.semaphore_signal(barrier, inc=1, device_id=sibling, device_id_type=MESH)

    codes_copy = pltpu.make_async_copy(codes_hbm, codes, in_s.at[0])
    hot_copy = pltpu.make_async_copy(hot_hbm, hot, in_s.at[1])
    rows_copy = pltpu.make_async_copy(rows_hbm, rows, in_s.at[2])
    old_copy = pltpu.make_async_copy(cb_hbm.at[:, pl.ds(pl.multiple_of(r * 256, 256), 256)], old, in_s.at[3])
    for copy in (codes_copy, hot_copy, rows_copy, old_copy):
        copy.start()
    hot_copy.wait()
    codes_copy.wait()

    def down(row):
        return jnp.transpose(jnp.broadcast_to(row, (128, 128)))

    hot_f = hot[...].astype(F32)
    hot_id = jnp.concatenate([down(hot_f[0:1, :128]), down(hot_f[0:1, 128:])], axis=0).astype(I32)
    hot_to = jnp.concatenate([down(hot_f[1:2, :128]), down(hot_f[1:2, 128:])], axis=0) + 1.0
    def order(owner):
        dx = lax.rem(owner + (4 - x), 4)
        dy = lax.rem(owner // 4 + (4 - y), 4)
        dz = lax.rem(owner // 16 + (4 - z), 4)
        ey, ez = dy - dy // 3, dz - dz // 3
        near = ez * 9 + ey * 3 + dx - dx // 3
        far = jnp.where(dz == 2, dy * 4 + dx, jnp.where(dy == 2, 16 + ez * 4 + dx, 28 + ez * 3 + ey))
        return jnp.where((dx == 2) | (dy == 2) | (dz == 2), NEAR + far, near)

    odd = lax.rem(iota((LANES, 128), 1), 2) == 1
    before = jnp.where(iota((128, 128), 0) < iota((128, 128), 1), 1.0, 0.0).astype(BF16)
    owner_id = iota((OWNERS, 128), 0)
    carry = jnp.zeros((OWNERS, 128), F32)
    for b in range(LANES):
        hit = jnp.where(hot_id == codes[b:b + 1, :], hot_to, 0.0)
        split[0, b:b + 1, :] = jnp.sum(hit, axis=0, keepdims=True)
    partner = split[0]
    code = jnp.where(odd & (partner > 0.0), partner.astype(I32) - 1, codes[...])
    owner = code // KB
    split[1] = owner.astype(F32)
    split[2] = (code - owner * KB).astype(F32)
    split[3] = order(owner).astype(F32)
    for b in range(LANES):
        lanes = slice(b * 128, (b + 1) * 128)
        owner = split[1, b:b + 1, :]
        mark = jnp.where(owner_id.astype(F32) == owner, 1.0, 0.0)
        ahead = jnp.dot(mark.astype(BF16), before, preferred_element_type=F32) + carry
        rank = jnp.sum(mark * ahead, axis=0, keepdims=True)
        carry = carry + jnp.sum(mark, axis=1, keepdims=True)
        rowbuf[0:1, lanes] = owner * SLOTS + rank
        rowbuf[1:2, lanes] = owner
        rowbuf[2:3, lanes] = rank
        rowbuf[3:4, lanes] = split[2, b:b + 1, :]
        rowbuf[4:5, lanes] = split[3, b:b + 1, :] * SLOTS + rank
    for u in range(3):
        r1[u][:, :, :, SLOTS:, :] = jnp.zeros((4, 4, 4, PITCH - SLOTS, WIDTH[u]), BF16)

    one, zero = jnp.ones((), BF16), jnp.zeros((), BF16)
    slot_iota = (iota((GS, 128), 0) - GS // 2).astype(F32).astype(BF16)

    def slot_rows(group, kind):
        middle = (group * GS + GS // 2).astype(F32)
        tiles = []
        for b in range(LANES):
            v = jnp.broadcast_to(rowbuf[kind:kind + 1, b * 128:(b + 1) * 128] - middle, (16, 128)).astype(BF16)
            v = jnp.concatenate([v] * (GS // 16), axis=0)
            tiles.append(jnp.where(v == slot_iota, one, zero))
        return jnp.concatenate(tiles, axis=1)

    rows_copy.wait()
    pl.semaphore_wait(barrier, 10)
    def remote(src, dst, ss, rs, to):
        return pltpu.make_async_remote_copy(src, dst, ss, rs, device_id=to, device_id_type=MESH)

    s1_copies = {}
    for u in range(3):
        for k in range(1, 4):
            to, there = peer(u, 0, k)
            s1_copies[u, k] = remote(
                pk[u].at[there], r1[u].at[:, :, k, pl.ds(0, SLOTS)], rs_s.at[u, 0, k],
                rs_r.at[u, 0, k], to)

    def send_half(oz, half, away, core):
        part = pl.ds(2 * half, 2)
        slots = pl.ds(0, SLOTS)
        for u in range(3):
            first = (u + core) % 3
            if first == 2:
                dz = lax.rem(oz - z + 4, 4)
                src, dst = pk[u].at[oz, :, part], r1[u].at[:, part, dz, slots]

                @pl.when(away)
                def _():
                    remote(src, dst, rs_s.at[u, 0, dz], rs_r.at[u, 0, dz], (d + (oz - z) * 16, r)).start()

                @pl.when(jnp.logical_not(away))
                def _():
                    pltpu.make_async_copy(src, dst, rs_r.at[u, 0, 0]).start()
                continue
            for k in (2, 1, 3, 0):
                to, there = peer(u, 0, k)

                def send(src, dst):
                    if k:
                        remote(src, dst, rs_s.at[u, 0, k], rs_r.at[u, 0, k], to).start()
                    else:
                        pltpu.make_async_copy(src, dst, rs_r.at[u, 0, 0]).start()

                if first == 0:
                    send(pk[u].at[there, part, oz], r1[u].at[part, oz, k, slots])
                else:
                    @pl.when(there // 2 == half)
                    def _():
                        send(pk[u].at[there, oz], r1[u].at[oz, :, k, slots])

    def pack(step, _):
        oz = lax.rem(z + 2 + 3 * step, 4)
        for half in range(2):
            packed = jnp.dot(slot_rows(oz * 2 + half, 0), rows[...], preferred_element_type=F32).astype(BF16)
            for j in range(GROUP):
                where = (j % 4, half * 2 + j // 4, oz)
                for u in range(3):
                    c1, c2, c3 = digits(where, u)
                    pk[u][c1, c2, c3] = packed[j * SLOTS:(j + 1) * SLOTS, COL[u]:COL[u] + WIDTH[u]]
            for core in range(2):
                @pl.when(r == core)
                def _():
                    send_half(oz, half, oz != z, core)
        return 0

    lax.fori_loop(0, 4, pack, 0)

    o = rowbuf[1:2, :].astype(I32)
    coords = (lax.rem(o, 4), lax.rem(o // 4, 4), o // 16)

    def lane_tiles(f):
        return jnp.concatenate([f(slice(b * 128, (b + 1) * 128)) for b in range(LANES)], axis=1)

    id128 = iota((128, 128), 0).astype(F32)
    rank_mark = lane_tiles(lambda s: jnp.where(rowbuf[2:3, s] == id128, 1.0, 0.0).astype(BF16))
    low_mark = lane_tiles(lambda s: jnp.where(rowbuf[3:4, s] == id128, 1.0, 0.0).astype(BF16))

    sc_copies, cn_copies = {}, {}
    for u in range(3):
        c1, c2, c3 = digits(coords, u)
        place = c1 * 16 + c2 * 4 + c3
        low = lane_tiles(lambda s: jnp.where(place[:, s] == owner_id, rowbuf[3:4, s] + 1.0, 0.0).astype(BF16))
        sc = lax.dot_general(low, rank_mark, NT, preferred_element_type=F32).astype(BF16)
        for c in range(4):
            sc_send[u, c] = sc[c * 16:(c + 1) * 16]
        for k in range(1, 4):
            to, there = peer(u, 0, k)
            sc_copies[u, k] = remote(sc_send.at[u, there], sc_recv.at[u, k], sc_s.at[u, k], sc_r.at[u, k], to)
            sc_copies[u, k].start()
        if u == 0:
            own = lane_tiles(lambda s: jnp.where(place[:, s] == owner_id, 1.0, 0.0).astype(BF16))
            cn = lax.dot_general(own, low_mark, NT, preferred_element_type=F32)
            for c in range(4):
                cn1[c] = cn[c * 16:(c + 1) * 16]
            for k in range(1, 4):
                to, there = peer(0, 0, k)
                cn_copies[0, k] = remote(cn1.at[there], cr1.at[k], cn_s.at[0, k], cn_r.at[0, k], to)
                cn_copies[0, k].start()

    low_wide = lane_tiles(
        lambda s: jnp.concatenate([jnp.broadcast_to(rowbuf[3:4, s] + 1.0, (16, 128)).astype(BF16)] * 8, axis=0))

    def slot_code(g, _):
        slot[0, pl.ds(g * GS, GS)] = lax.dot_general(
            slot_rows(g, 4), low_wide, NT, preferred_element_type=F32).astype(BF16)
        return 0

    lax.fori_loop(0, NG, slot_code, 0)
    slot_copy = remote(slot.at[0], slot.at[1], x_s.at[3], x_r.at[3], sibling)
    slot_copy.start()
    for b in range(LANES):
        v = jnp.broadcast_to(rowbuf[4:5, b * 128:(b + 1) * 128], (128, 128))
        vcol[b * 128:(b + 1) * 128, :] = jnp.transpose(v)

    code_id = (iota((KB, 256), 0) + 1).astype(F32)
    s2_copies, s3_copies = {}, {}
    def ring_sum(u, q, t):
        there = peer(u, 1, q)[1]
        mark = jnp.where(code_id == crow[u, pl.ds(there * 4 + t, 1), :], 1.0, 0.0).astype(BF16)
        return jnp.dot(mark, r1[u][there, t].reshape(4 * PITCH, WIDTH[u]), preferred_element_type=F32)

    def send_sum(u, name, src, dst, lane, k):
        s2_copies[(u,) + name] = remote(src, dst, w_s.at[u, lane], w_r.at[u, lane], peer(u, 1, k)[0])
        s2_copies[(u,) + name].start()

    halves = (pl.ds(0, 2), pl.ds(2, 2))
    for u in (1, 2, 0):
        c1, c2, c3 = my_digits[u]
        pltpu.make_async_copy(pk[u].at[c1], r1[u].at[:, :, 0, pl.ds(0, SLOTS)],
                              rs_r.at[u, 0, 0]).wait()
        for k in range(1, 4):
            s1_copies[u, k].wait_recv()
            sc_copies[u, k].wait_recv()
        quarter = [sc_send[u, c1].astype(F32)] + [sc_recv[u, k].astype(F32) for k in range(1, 4)]
        crow[u, :, 0:128] = quarter[0] + pltpu.roll(quarter[1], 64, 1)
        crow[u, :, 128:256] = quarter[2] + pltpu.roll(quarter[3], 64, 1)
        parts = [ring_sum(u, 2, t).astype(BF16) for t in range(4)]
        for t in range(4):
            s2[u][1, t] = parts[t]
        for half in range(2):
            send_sum(u, ("via", half), s2[u].at[1, halves[half]], t2[u].at[half], half, (1, 3)[half])
    for u in (1, 2, 0):
        order2 = ((1, 2), (1, 3), (3, 0), (3, 1))
        parts = [ring_sum(u, q, t).astype(BF16) for q, t in order2]
        for (q, t), part in zip(order2, parts):
            s2[u][q - 1, t] = part
        for half, q in ((1, 1), (0, 3)):
            send_sum(u, ("whole", q), s2[u].at[q - 1, halves[half]], r2[u].at[q // 2, halves[half]], 2 + q // 2, q)
    u, c1 = 0, my_digits[0][0]
    total = cn1[c1]
    for k in range(1, 4):
        cn_copies[0, k].wait_recv()
        total = total + cr1[k]
    cn2[...] = total
    for k in range(1, 4):
        cn_copies[1, k] = remote(cn2, cr2.at[k - 1], cn_s.at[1, k], cn_r.at[1, k], peer(0, 1, k)[0])
        cn_copies[1, k].start()

    for u in (1, 2, 0):
        for half, q in ((0, 1), (1, 3)):
            parts = [ring_sum(u, q, 2 * half + t) for t in range(2)]
            s2_copies[u, "via", half].wait_recv()
            for t in range(2):
                s2[u][q - 1, 2 * half + t] = (parts[t] + t2[u][half, t].astype(F32)).astype(BF16)
            send_sum(u, ("added", q), s2[u].at[q - 1, halves[half]], r2[u].at[q // 2, halves[half]], 4 + q // 2, q)
    for u in (1, 2, 0):
        for t in range(4):
            own2[u][t] = ring_sum(u, 0, t)

    for u in (1, 2, 0):
        for name in ("whole", "added"):
            for q in (1, 3):
                s2_copies[u, name, q].wait_recv()
        for q in (1, 3, 2, 0):
            to, there = peer(u, 2, q)
            part = own2[u][there]
            for k in range(2):
                part = part + r2[u][k, there].astype(F32)
            if q == 0:
                acc3[u][...] = part
            else:
                s3[u][q - 1] = part.astype(BF16)
                s3_copies[u, q] = remote(s3[u].at[q - 1], r3[u].at[q - 1], rs_s.at[u, 2, q], rs_r.at[u, 2, q], to)
                s3_copies[u, q].start()
        if u == 0:
            total = cn2[...]
            for k in range(1, 4):
                cn_copies[1, k].wait_recv()
                total = total + cr2[k - 1]
            cn3[...] = total
            for k in range(1, 4):
                cn_copies[2, k] = remote(cn3, cr3.at[k - 1], cn_s.at[2, k], cn_r.at[2, k], peer(0, 2, k)[0])
                cn_copies[2, k].start()

    for u in (1, 2, 0):
        part = acc3[u][...]
        for q in range(1, 4):
            s3_copies[u, q].wait_recv()
            part = part + r3[u][q - 1].astype(F32)
        if u == 0:
            tot3[0] = part
        else:
            tot3[1, :, (u - 1) * 128:u * 128] = part
    total = cn3[...]
    for k in range(1, 4):
        cn_copies[2, k].wait_recv()
        total = total + cr3[k - 1]
    mine_at = my_digits[0][1] * 4 + my_digits[0][2]
    cx[...] = jnp.broadcast_to(
        jnp.sum(jnp.where(iota((16, 128), 0) == mine_at, total, 0.0), axis=0, keepdims=True), (8, 128))
    tot_copy = remote(tot3.at[1 - r], tot3r, x_s.at[0], x_r.at[0], sibling)
    cx_copy = remote(cx, cxr, x_s.at[1], x_r.at[1], sibling)
    cx_copy.start()
    tot_copy.start()
    cx_copy.wait_recv()
    count = cx[0:1, :] + cxr[0:1, :]
    diagonal = iota((128, 128), 0) == iota((128, 128), 1)
    count = jnp.sum(jnp.where(diagonal, jnp.broadcast_to(count, (128, 128)), 0.0), axis=1, keepdims=True)
    old_copy.wait()
    tot_copy.wait_recv()
    new = (tot3[r] + tot3r[...] + PRIOR * old[...]) / (count + PRIOR)
    low_new = new.astype(BF16)
    for u in range(3):
        c1, c2, c3 = my_digits[u]
        tb[u][c1, c2, c3] = low_new[CUT[u][0]:CUT[u][0] + CUT[u][1]]
    nb[0] = new[:64]
    nb[1] = new[64:]

    ag = {}

    def gather(u, stage, tag, k, block, lane):
        copy = remote(block, block, ag_s.at[u, lane], ag_r.at[u, lane], peer(u, stage, k)[0])
        copy.start()
        ag[(u,) + tag] = copy

    def line(u, e1, e2, half=None):
        c1, c2, c3 = my_digits[u]
        i1, i2 = lax.rem(c1 + e1, 4), lax.rem(c2 + e2, 4)
        return tb[u].at[i1, i2] if half is None else tb[u].at[i1, i2, pl.ds(2 * half, 2)]

    def both_ways(u, stage, tag, block, lane):
        gather(u, stage, tag + (1,), 1, block, lane)
        gather(u, stage, tag + (3,), 3, block, lane + 1)

    def pass_on(u, stage, tag, e1, e2, lane):
        step = {0: ((e1 + 3) % 4, (e1 + 1) % 4, e2, e2), 1: (e1, e1, (e2 + 3) % 4, (e2 + 1) % 4)}[stage]
        ag[(u,) + tag + (1,)].wait_recv()
        gather(u, stage, tag + ("up",), 1, line(u, step[0], step[2], 0), lane + 2)
        ag[(u,) + tag + (3,)].wait_recv()
        gather(u, stage, tag + ("down",), 3, line(u, step[1], step[3], 1), lane + 3)

    for u in range(3):
        c1, c2, c3 = my_digits[u]
        for k in range(1, 4):
            gather(u, 2, ("a", k), k, tb[u].at[c1, c2, c3], k - 1)
    new_copy = remote(nb.at[1 - r], nbr, x_s.at[2], x_r.at[2], sibling)
    new_copy.start()
    for u in range(3):
        for k in range(1, 4):
            ag[u, "a", k].wait_recv()
        both_ways(u, 1, ("b",), line(u, 0, 0), 4)
        both_ways(u, 0, ("c", 0), line(u, 0, 0), 8)
    new_copy.wait_recv()
    kept = nb[r]
    new_out[:, :256] = jnp.where(r == 0, kept, nbr[...])
    new_out[:, 256:] = jnp.where(r == 0, nbr[...], kept)
    new_out_copy = pltpu.make_async_copy(new_out, newcb, out_s.at[2])
    new_out_copy.start()
    for u in range(3):
        pass_on(u, 1, ("b",), 0, 0, 4)
        both_ways(u, 0, ("c", 1), line(u, 0, 1), 12)
        both_ways(u, 0, ("c", 3), line(u, 0, 3), 16)
    for u in range(3):
        pass_on(u, 0, ("c", 0), 0, 0, 8)
    for u in range(3):
        ag[u, "b", "up"].wait_recv()
        ag[u, "b", "down"].wait_recv()
        both_ways(u, 0, ("c", 2), line(u, 0, 2), 20)
    for u in range(3):
        pass_on(u, 0, ("c", 1), 0, 1, 12)
        pass_on(u, 0, ("c", 3), 0, 3, 16)
    slot_copy.wait_recv()

    lane_code = (iota((SLOTS, 128), 1) + 1).astype(F32).astype(BF16)

    def take(first, steps, sem):
        for begin in range(0, len(steps), 3):
            found = []
            for j in range(begin, min(begin + 3, len(steps))):
                where = tuple(lax.rem(c + e, 4) for c, e in zip(mine, steps[j]))
                parts = []
                for u in range(3):
                    c1, c2, c3 = digits(where, u)
                    parts.append(tb[u][c1, c2, c3])
                at = pl.ds((first + j) * SLOTS, SLOTS)
                mark = jnp.concatenate([jnp.where(slot[i, at] == lane_code, one, zero) for i in range(2)], axis=0)
                got = jnp.dot(mark, jnp.concatenate(parts, axis=0), preferred_element_type=F32)
                found.append((at, got.astype(BF16)))
            for at, got in found:
                picks[r, at] = got[:SLOTS]
                psend[at] = got[SLOTS:]
        at = pl.ds(first * SLOTS, len(steps) * SLOTS)
        remote(psend.at[at], picks.at[r, at], p_s.at[sem], p_r.at[sem], sibling).start()

    def near(ez, _):
        take(ez * 9, [((0, 1, 3)[i % 3], (0, 1, 3)[i // 3], ez + ez // 2) for i in range(9)], 0)
        return 0

    lax.fori_loop(0, 3, near, 0)
    for u in range(3):
        pass_on(u, 0, ("c", 2), 0, 2, 20)

    def slot_marks(at, begin, end):
        v = vcol[at, :]
        tiles = []
        for g in range(begin // GROUP, end // GROUP):
            w = (v - (g * GS + GS // 2)).astype(BF16)
            for t in range(GS // 128):
                tiles.append(jnp.where(w == lane_slot[t], one, zero))
        return jnp.concatenate(tiles, axis=1)

    lane_slot = [(iota((BLOCK, 128), 1) + (128 * t - GS // 2)).astype(F32).astype(BF16) for t in range(GS // 128)]
    near_rows = pl.ds(0, NEAR * SLOTS)
    far_rows = pl.ds(NEAR * SLOTS, (OWNERS - NEAR) * SLOTS)
    p_copies = [remote(psend.at[at], picks.at[1 - r, at], p_s.at[i], p_r.at[i], sibling)
                for i, at in enumerate((near_rows, far_rows))]
    p_copies[0].wait_recv()

    def unpack_near(m, _):
        at = pl.ds(m * BLOCK, BLOCK)
        mark = slot_marks(at, 0, NEAR_KEPT)
        for h in range(2):
            got = jnp.dot(mark, picks[h, 0:NEAR_KEPT * SLOTS], preferred_element_type=F32)
            held[h, at] = got.astype(BF16)
        return 0

    lax.fori_loop(0, ROWS // BLOCK, unpack_near, 0)
    for u in range(3):
        for e in range(4):
            ag[u, "c", e, "up"].wait_recv()
            ag[u, "c", e, "down"].wait_recv()

    def far_z(dy, _):
        take(NEAR + dy * 4, [(i, dy, 2) for i in range(4)], 1)
        return 0

    def far_y(ez, _):
        take(NEAR + 16 + ez * 4, [(i, 2, ez + ez // 2) for i in range(4)], 1)
        return 0

    def far_x(ez, _):
        take(NEAR + 28 + ez * 3, [(2, (0, 1, 3)[i], ez + ez // 2) for i in range(3)], 1)
        return 0

    lax.fori_loop(0, 4, far_z, 0)
    lax.fori_loop(0, 3, far_y, 0)
    lax.fori_loop(0, 3, far_x, 0)

    outs = []
    for turn in range(2):
        h = r + turn * (1 - 2 * r)
        cols = pl.ds(pl.multiple_of(h * 256, 256), 256)
        if turn:
            p_copies[1].wait_recv()

        def unpack(m, _):
            at = pl.ds(m * BLOCK, BLOCK)
            mark = slot_marks(at, NEAR_KEPT, OWNERS)
            got = jnp.dot(mark, picks[h, NEAR_KEPT * SLOTS:], preferred_element_type=F32)
            got = got + held[h, at].astype(F32)
            out[h, at] = (rows[at, cols].astype(F32) - got).astype(BF16)
            pltpu.make_async_copy(out.at[h, at], res.at[at, cols], out_s.at[turn]).start()
            return 0

        lax.fori_loop(0, ROWS // BLOCK, unpack, 0)
        outs.append(pltpu.make_async_copy(out.at[h], res.at[:, cols], out_s.at[turn]))
    new_out_copy.wait()
    for copy in outs:
        copy.wait()

    for group in (s1_copies, sc_copies, cn_copies, s2_copies, s3_copies, ag):
        for copy in group.values():
            copy.wait_send()
    for copy in [tot_copy, cx_copy, new_copy, slot_copy] + p_copies:
        copy.wait_send()


def hand_over(new, residual):
    parts = 8

    def copy(new_in, res_in, new_out, res_out, new_buf, res_buf, sems):
        def moves(i):
            if i == parts:
                return (pltpu.make_async_copy(new_in, new_buf, sems.at[0, i]),
                        pltpu.make_async_copy(new_buf, new_out, sems.at[1, i]))
            at = pl.ds(i * (ROWS // parts), ROWS // parts)
            return (pltpu.make_async_copy(res_in.at[at], res_buf.at[at], sems.at[0, i]),
                    pltpu.make_async_copy(res_buf.at[at], res_out.at[at], sems.at[1, i]))

        pairs = [moves(i) for i in range(parts + 1)]
        for there, _ in pairs:
            there.start()
        for there, back in pairs:
            there.wait()
            back.start()
        for _, back in pairs:
            back.wait()

    anywhere = pl.BlockSpec(memory_space=pl.ANY)
    return pl.pallas_call(
        copy,
        out_shape=(jax.ShapeDtypeStruct(new.shape, new.dtype), jax.ShapeDtypeStruct(residual.shape, residual.dtype)),
        in_specs=[anywhere] * 2,
        out_specs=(anywhere, anywhere),
        scratch_shapes=[pltpu.VMEM(new.shape, new.dtype), pltpu.VMEM(residual.shape, residual.dtype),
                        pltpu.SemaphoreType.DMA((2, parts + 1))],
    )(new, residual)


def on_device(rows_in, row_codes, hot_split, codebook):
    vm = pltpu.VMEM
    dma = pltpu.SemaphoreType.DMA
    anywhere = pl.BlockSpec(memory_space=pl.ANY)
    scratch = [
        vm((ROWS, E), BF16),
        vm((LANES, 128), I32),
        vm((2, 256), I32),
        vm((KB, 256), F32),
        vm((KB // 2, E), F32),
        tuple(vm((4, 4, 4, SLOTS, w), BF16) for w in WIDTH),
        tuple(vm((4, 4, 4, PITCH, w), BF16) for w in WIDTH),
        vm((3, 16, 256), F32),
        tuple(vm((3, 4, KB, w), BF16) for w in WIDTH),
        tuple(vm((2, 2, KB, w), BF16) for w in WIDTH),
        tuple(vm((4, KB, w), F32) for w in WIDTH),
        tuple(vm((2, 4, KB, w), BF16) for w in WIDTH),
        tuple(vm((3, KB, w), BF16) for w in WIDTH),
        tuple(vm((KB, w), F32) for w in WIDTH),
        tuple(vm((3, KB, w), BF16) for w in WIDTH),
        tuple(vm((4, 4, 4, n, 256), BF16) for _, n in CUT),
        vm((4, LANES, 128), F32),
        vm((8, ROWS), F32),
        vm((ROWS, 128), F32),
        vm((3, 4, 16, 128), BF16),
        vm((3, 4, 16, 128), BF16),
        vm((4, 16, 128), F32),
        vm((4, 16, 128), F32),
        vm((16, 128), F32),
        vm((3, 16, 128), F32),
        vm((16, 128), F32),
        vm((3, 16, 128), F32),
        vm((8, 128), F32),
        vm((8, 128), F32),
        vm((2, KB, 256), F32),
        vm((KB, 256), F32),
        vm((2, 64, 256), F32),
        vm((64, 256), F32),
        vm((2, OWNERS * SLOTS, 128), BF16),
        vm((2, OWNERS * SLOTS, 256), BF16),
        vm((OWNERS * SLOTS, 256), BF16),
        vm((2, ROWS, 256), BF16),
        vm((2, ROWS, 256), BF16),
        dma((4,)), dma((3,)),
        dma((3, 6)), dma((3, 6)),
        dma((3, 3, 4)), dma((3, 3, 4)),
        dma((3, 4)), dma((3, 4)),
        dma((3, 4)), dma((3, 4)),
        dma((3, 24)), dma((3, 24)),
        dma((4,)), dma((4,)),
        dma((2,)), dma((2,)),
    ]
    new, residual = pl.pallas_call(
        kernel,
        out_shape=(jax.ShapeDtypeStruct((KB // 2, E), F32), jax.ShapeDtypeStruct((ROWS, E), BF16)),
        in_specs=[anywhere] * 4,
        out_specs=(anywhere, anywhere),
        scratch_shapes=scratch,
        compiler_params=pltpu.CompilerParams(collective_id=0, has_side_effects=True,
                                             vmem_limit_bytes=56 * 2**20),
    )(rows_in, row_codes.reshape(LANES, 128), hot_split.T, codebook)
    return hand_over(new, residual)


def solution(mesh):
    return jax.shard_map(
        on_device,
        mesh=mesh,
        in_specs=(P(("dp", "rep"), None), P(("dp", "rep")), P(), P("dp", None)),
        out_specs=(P(("dp", "rep"), None), P(("dp", "rep"), None)),
        check_vma=False,
    )
```

```python
import jax
import jax.numpy as jnp
from jax import lax
from jax.experimental import pallas as pl
from jax.experimental.pallas import tpu as pltpu
from jax.sharding import PartitionSpec as P

MESH = pl.DeviceIdType.MESH
F32, BF16, I32 = jnp.float32, jnp.bfloat16, jnp.int32

PRIOR = 8.0
ROWS = 2048
E = 512
KB = 128
BLOCK = 1024
OWNERS = 64
SLOTS = 48
PITCH = 64
GROUP = 8
GS = GROUP * SLOTS
NG = OWNERS // GROUP
LANES = ROWS // 128

WIDTH = (256, 128, 128)
COL = (0, 256, 384)
CUT = ((0, 48), (48, 48), (96, 32))

NEAR = 27
NEAR_KEPT = 24

NT = (((1,), (1,)), ((), ()))


def iota(shape, dim):
    return lax.broadcasted_iota(I32, shape, dim)


def kernel(rows_hbm, codes_hbm, hot_hbm, cb_hbm, newcb, res, rows, codes, hot, old, new_out, pk, r1, crow, s2, t2, own2, r2, s3, acc3, r3, tb,
           split, rowbuf, vcol, sc_send, sc_recv, cn1, cr1, cn2, cr2, cn3, cr3, cx, cxr,
           tot3, tot3r, nb, nbr, slot, picks, psend, held, out,
           in_s, out_s, w_s, w_r, rs_s, rs_r, sc_s, sc_r, cn_s, cn_r, ag_s, ag_r, x_s, x_r, p_s, p_r):
    d = lax.axis_index("dp")
    r = lax.axis_index("rep")
    x, y, z = lax.rem(d, 4), lax.rem(d // 4, 4), d // 16
    mine = (x, y, z)
    stride = (1, 4, 16)
    sibling = (d, 1 - r)

    def pick(seq, u, stage):
        a, b = seq[(u + stage) % 3], seq[(u + stage + 1) % 3]
        return a + r * (b - a)

    def digits(coords, u):
        return tuple(pick(coords, u, stage) for stage in range(3))

    def peer(u, stage, k):
        c = pick(mine, u, stage)
        there = lax.rem(c + k, 4)
        return (d + (there - c) * pick(stride, u, stage), r), there

    my_digits = [digits(mine, u) for u in range(3)]

    barrier = pltpu.get_barrier_semaphore()
    for axis in range(3):
        for k in range(1, 4):
            there = lax.rem(mine[axis] + k, 4)
            pl.semaphore_signal(barrier, inc=1, device_id=(d + (there - mine[axis]) * stride[axis], r),
                                device_id_type=MESH)
    pl.semaphore_signal(barrier, inc=1, device_id=sibling, device_id_type=MESH)

    codes_copy = pltpu.make_async_copy(codes_hbm, codes, in_s.at[0])
    hot_copy = pltpu.make_async_copy(hot_hbm, hot, in_s.at[1])
    rows_copy = pltpu.make_async_copy(rows_hbm, rows, in_s.at[2])
    old_copy = pltpu.make_async_copy(cb_hbm.at[:, pl.ds(pl.multiple_of(r * 256, 256), 256)], old, in_s.at[3])
    for copy in (codes_copy, hot_copy, rows_copy, old_copy):
        copy.start()
    hot_copy.wait()
    codes_copy.wait()

    def down(row):
        return jnp.transpose(jnp.broadcast_to(row, (128, 128)))

    hot_f = hot[...].astype(F32)
    hot_id = jnp.concatenate([down(hot_f[0:1, :128]), down(hot_f[0:1, 128:])], axis=0).astype(I32)
    hot_to = jnp.concatenate([down(hot_f[1:2, :128]), down(hot_f[1:2, 128:])], axis=0) + 1.0
    def order(owner):
        dx = lax.rem(owner + (4 - x), 4)
        dy = lax.rem(owner // 4 + (4 - y), 4)
        dz = lax.rem(owner // 16 + (4 - z), 4)
        ey, ez = dy - dy // 3, dz - dz // 3
        near = ez * 9 + ey * 3 + dx - dx // 3
        far = jnp.where(dz == 2, dy * 4 + dx, jnp.where(dy == 2, 16 + ez * 4 + dx, 28 + ez * 3 + ey))
        return jnp.where((dx == 2) | (dy == 2) | (dz == 2), NEAR + far, near)

    odd = lax.rem(iota((LANES, 128), 1), 2) == 1
    before = jnp.where(iota((128, 128), 0) < iota((128, 128), 1), 1.0, 0.0).astype(BF16)
    owner_id = iota((OWNERS, 128), 0)
    carry = jnp.zeros((OWNERS, 128), F32)
    for b in range(LANES):
        hit = jnp.where(hot_id == codes[b:b + 1, :], hot_to, 0.0)
        split[0, b:b + 1, :] = jnp.sum(hit, axis=0, keepdims=True)
    partner = split[0]
    code = jnp.where(odd & (partner > 0.0), partner.astype(I32) - 1, codes[...])
    owner = code // KB
    split[1] = owner.astype(F32)
    split[2] = (code - owner * KB).astype(F32)
    split[3] = order(owner).astype(F32)
    for b in range(LANES):
        lanes = slice(b * 128, (b + 1) * 128)
        owner = split[1, b:b + 1, :]
        mark = jnp.where(owner_id.astype(F32) == owner, 1.0, 0.0)
        ahead = jnp.dot(mark.astype(BF16), before, preferred_element_type=F32) + carry
        rank = jnp.sum(mark * ahead, axis=0, keepdims=True)
        carry = carry + jnp.sum(mark, axis=1, keepdims=True)
        rowbuf[0:1, lanes] = owner * SLOTS + rank
        rowbuf[1:2, lanes] = owner
        rowbuf[2:3, lanes] = rank
        rowbuf[3:4, lanes] = split[2, b:b + 1, :]
        rowbuf[4:5, lanes] = split[3, b:b + 1, :] * SLOTS + rank
    for u in range(3):
        r1[u][:, :, :, SLOTS:, :] = jnp.zeros((4, 4, 4, PITCH - SLOTS, WIDTH[u]), BF16)

    one, zero = jnp.ones((), BF16), jnp.zeros((), BF16)
    slot_iota = (iota((GS, 128), 0) - GS // 2).astype(F32).astype(BF16)

    def slot_rows(group, kind):
        middle = (group * GS + GS // 2).astype(F32)
        tiles = []
        for b in range(LANES):
            v = jnp.broadcast_to(rowbuf[kind:kind + 1, b * 128:(b + 1) * 128] - middle, (16, 128)).astype(BF16)
            v = jnp.concatenate([v] * (GS // 16), axis=0)
            tiles.append(jnp.where(v == slot_iota, one, zero))
        return jnp.concatenate(tiles, axis=1)

    rows_copy.wait()
    pl.semaphore_wait(barrier, 10)
    def remote(src, dst, ss, rs, to):
        return pltpu.make_async_remote_copy(src, dst, ss, rs, device_id=to, device_id_type=MESH)

    s1_copies = {}
    for u in range(3):
        for k in range(1, 4):
            to, there = peer(u, 0, k)
            s1_copies[u, k] = remote(
                pk[u].at[there], r1[u].at[:, :, k, pl.ds(0, SLOTS)], rs_s.at[u, 0, k],
                rs_r.at[u, 0, k], to)

    def send_half(oz, half, away, core):
        part = pl.ds(2 * half, 2)
        slots = pl.ds(0, SLOTS)
        for u in range(3):
            first = (u + core) % 3
            if first == 2:
                dz = lax.rem(oz - z + 4, 4)
                src, dst = pk[u].at[oz, :, part], r1[u].at[:, part, dz, slots]

                @pl.when(away)
                def _():
                    remote(src, dst, rs_s.at[u, 0, dz], rs_r.at[u, 0, dz], (d + (oz - z) * 16, r)).start()

                @pl.when(jnp.logical_not(away))
                def _():
                    pltpu.make_async_copy(src, dst, rs_r.at[u, 0, 0]).start()
                continue
            for k in (2, 1, 3, 0):
                to, there = peer(u, 0, k)

                def send(src, dst):
                    if k:
                        remote(src, dst, rs_s.at[u, 0, k], rs_r.at[u, 0, k], to).start()
                    else:
                        pltpu.make_async_copy(src, dst, rs_r.at[u, 0, 0]).start()

                if first == 0:
                    send(pk[u].at[there, part, oz], r1[u].at[part, oz, k, slots])
                else:
                    @pl.when(there // 2 == half)
                    def _():
                        send(pk[u].at[there, oz], r1[u].at[oz, :, k, slots])

    def pack(step, _):
        oz = lax.rem(z + 2 + 3 * step, 4)
        for half in range(2):
            packed = jnp.dot(slot_rows(oz * 2 + half, 0), rows[...], preferred_element_type=F32).astype(BF16)
            for j in range(GROUP):
                where = (j % 4, half * 2 + j // 4, oz)
                for u in range(3):
                    c1, c2, c3 = digits(where, u)
                    pk[u][c1, c2, c3] = packed[j * SLOTS:(j + 1) * SLOTS, COL[u]:COL[u] + WIDTH[u]]
            for core in range(2):
                @pl.when(r == core)
                def _():
                    send_half(oz, half, oz != z, core)
        return 0

    lax.fori_loop(0, 4, pack, 0)

    o = rowbuf[1:2, :].astype(I32)
    coords = (lax.rem(o, 4), lax.rem(o // 4, 4), o // 16)

    def lane_tiles(f):
        return jnp.concatenate([f(slice(b * 128, (b + 1) * 128)) for b in range(LANES)], axis=1)

    id128 = iota((128, 128), 0).astype(F32)
    rank_mark = lane_tiles(lambda s: jnp.where(rowbuf[2:3, s] == id128, 1.0, 0.0).astype(BF16))
    low_mark = lane_tiles(lambda s: jnp.where(rowbuf[3:4, s] == id128, 1.0, 0.0).astype(BF16))

    sc_copies, cn_copies = {}, {}
    for u in range(3):
        c1, c2, c3 = digits(coords, u)
        place = c1 * 16 + c2 * 4 + c3
        low = lane_tiles(lambda s: jnp.where(place[:, s] == owner_id, rowbuf[3:4, s] + 1.0, 0.0).astype(BF16))
        sc = lax.dot_general(low, rank_mark, NT, preferred_element_type=F32).astype(BF16)
        for c in range(4):
            sc_send[u, c] = sc[c * 16:(c + 1) * 16]
        for k in range(1, 4):
            to, there = peer(u, 0, k)
            sc_copies[u, k] = remote(sc_send.at[u, there], sc_recv.at[u, k], sc_s.at[u, k], sc_r.at[u, k], to)
            sc_copies[u, k].start()
        if u == 0:
            own = lane_tiles(lambda s: jnp.where(place[:, s] == owner_id, 1.0, 0.0).astype(BF16))
            cn = lax.dot_general(own, low_mark, NT, preferred_element_type=F32)
            for c in range(4):
                cn1[c] = cn[c * 16:(c + 1) * 16]
            for k in range(1, 4):
                to, there = peer(0, 0, k)
                cn_copies[0, k] = remote(cn1.at[there], cr1.at[k], cn_s.at[0, k], cn_r.at[0, k], to)
                cn_copies[0, k].start()

    low_wide = lane_tiles(
        lambda s: jnp.concatenate([jnp.broadcast_to(rowbuf[3:4, s] + 1.0, (16, 128)).astype(BF16)] * 8, axis=0))

    def slot_code(g, _):
        slot[0, pl.ds(g * GS, GS)] = lax.dot_general(
            slot_rows(g, 4), low_wide, NT, preferred_element_type=F32).astype(BF16)
        return 0

    lax.fori_loop(0, NG, slot_code, 0)
    slot_copy = remote(slot.at[0], slot.at[1], x_s.at[3], x_r.at[3], sibling)
    slot_copy.start()
    for b in range(LANES):
        v = jnp.broadcast_to(rowbuf[4:5, b * 128:(b + 1) * 128], (128, 128))
        vcol[b * 128:(b + 1) * 128, :] = jnp.transpose(v)

    code_id = (iota((KB, 256), 0) + 1).astype(F32)
    s2_copies, s3_copies = {}, {}
    def ring_sum(u, q, t):
        there = peer(u, 1, q)[1]
        mark = jnp.where(code_id == crow[u, pl.ds(there * 4 + t, 1), :], 1.0, 0.0).astype(BF16)
        return jnp.dot(mark, r1[u][there, t].reshape(4 * PITCH, WIDTH[u]), preferred_element_type=F32)

    def send_sum(u, name, src, dst, lane, k):
        s2_copies[(u,) + name] = remote(src, dst, w_s.at[u, lane], w_r.at[u, lane], peer(u, 1, k)[0])
        s2_copies[(u,) + name].start()

    halves = (pl.ds(0, 2), pl.ds(2, 2))
    for u in (1, 2, 0):
        c1, c2, c3 = my_digits[u]
        pltpu.make_async_copy(pk[u].at[c1], r1[u].at[:, :, 0, pl.ds(0, SLOTS)],
                              rs_r.at[u, 0, 0]).wait()
        for k in range(1, 4):
            s1_copies[u, k].wait_recv()
            sc_copies[u, k].wait_recv()
        quarter = [sc_send[u, c1].astype(F32)] + [sc_recv[u, k].astype(F32) for k in range(1, 4)]
        crow[u, :, 0:128] = quarter[0] + pltpu.roll(quarter[1], 64, 1)
        crow[u, :, 128:256] = quarter[2] + pltpu.roll(quarter[3], 64, 1)
        parts = [ring_sum(u, 2, t).astype(BF16) for t in range(4)]
        for t in range(4):
            s2[u][1, t] = parts[t]
        for half in range(2):
            send_sum(u, ("via", half), s2[u].at[1, halves[half]], t2[u].at[half], half, (1, 3)[half])
    for u in (1, 2, 0):
        order2 = ((1, 2), (1, 3), (3, 0), (3, 1))
        parts = [ring_sum(u, q, t).astype(BF16) for q, t in order2]
        for (q, t), part in zip(order2, parts):
            s2[u][q - 1, t] = part
        for half, q in ((1, 1), (0, 3)):
            send_sum(u, ("whole", q), s2[u].at[q - 1, halves[half]], r2[u].at[q // 2, halves[half]], 2 + q // 2, q)
    u, c1 = 0, my_digits[0][0]
    total = cn1[c1]
    for k in range(1, 4):
        cn_copies[0, k].wait_recv()
        total = total + cr1[k]
    cn2[...] = total
    for k in range(1, 4):
        cn_copies[1, k] = remote(cn2, cr2.at[k - 1], cn_s.at[1, k], cn_r.at[1, k], peer(0, 1, k)[0])
        cn_copies[1, k].start()

    for u in (1, 2, 0):
        for half, q in ((0, 1), (1, 3)):
            parts = [ring_sum(u, q, 2 * half + t) for t in range(2)]
            s2_copies[u, "via", half].wait_recv()
            for t in range(2):
                s2[u][q - 1, 2 * half + t] = (parts[t] + t2[u][half, t].astype(F32)).astype(BF16)
            send_sum(u, ("added", q), s2[u].at[q - 1, halves[half]], r2[u].at[q // 2, halves[half]], 4 + q // 2, q)
    for u in (1, 2, 0):
        for t in range(4):
            own2[u][t] = ring_sum(u, 0, t)

    for u in (1, 2, 0):
        for name in ("whole", "added"):
            for q in (1, 3):
                s2_copies[u, name, q].wait_recv()
        for q in (1, 3, 2, 0):
            to, there = peer(u, 2, q)
            part = own2[u][there]
            for k in range(2):
                part = part + r2[u][k, there].astype(F32)
            if q == 0:
                acc3[u][...] = part
            else:
                s3[u][q - 1] = part.astype(BF16)
                s3_copies[u, q] = remote(s3[u].at[q - 1], r3[u].at[q - 1], rs_s.at[u, 2, q], rs_r.at[u, 2, q], to)
                s3_copies[u, q].start()
        if u == 0:
            total = cn2[...]
            for k in range(1, 4):
                cn_copies[1, k].wait_recv()
                total = total + cr2[k - 1]
            cn3[...] = total
            for k in range(1, 4):
                cn_copies[2, k] = remote(cn3, cr3.at[k - 1], cn_s.at[2, k], cn_r.at[2, k], peer(0, 2, k)[0])
                cn_copies[2, k].start()

    for u in (1, 2, 0):
        part = acc3[u][...]
        for q in range(1, 4):
            s3_copies[u, q].wait_recv()
            part = part + r3[u][q - 1].astype(F32)
        if u == 0:
            tot3[0] = part
        else:
            tot3[1, :, (u - 1) * 128:u * 128] = part
    total = cn3[...]
    for k in range(1, 4):
        cn_copies[2, k].wait_recv()
        total = total + cr3[k - 1]
    mine_at = my_digits[0][1] * 4 + my_digits[0][2]
    cx[...] = jnp.broadcast_to(
        jnp.sum(jnp.where(iota((16, 128), 0) == mine_at, total, 0.0), axis=0, keepdims=True), (8, 128))
    tot_copy = remote(tot3.at[1 - r], tot3r, x_s.at[0], x_r.at[0], sibling)
    cx_copy = remote(cx, cxr, x_s.at[1], x_r.at[1], sibling)
    cx_copy.start()
    tot_copy.start()
    cx_copy.wait_recv()
    count = cx[0:1, :] + cxr[0:1, :]
    diagonal = iota((128, 128), 0) == iota((128, 128), 1)
    count = jnp.sum(jnp.where(diagonal, jnp.broadcast_to(count, (128, 128)), 0.0), axis=1, keepdims=True)
    old_copy.wait()
    tot_copy.wait_recv()
    new = (tot3[r] + tot3r[...] + PRIOR * old[...]) / (count + PRIOR)
    low_new = new.astype(BF16)
    for u in range(3):
        c1, c2, c3 = my_digits[u]
        tb[u][c1, c2, c3] = low_new[CUT[u][0]:CUT[u][0] + CUT[u][1]]
    nb[0] = new[:64]
    nb[1] = new[64:]

    ag = {}

    def gather(u, stage, tag, k, block, lane):
        copy = remote(block, block, ag_s.at[u, lane], ag_r.at[u, lane], peer(u, stage, k)[0])
        copy.start()
        ag[(u,) + tag] = copy

    def line(u, e1, e2, half=None):
        c1, c2, c3 = my_digits[u]
        i1, i2 = lax.rem(c1 + e1, 4), lax.rem(c2 + e2, 4)
        return tb[u].at[i1, i2] if half is None else tb[u].at[i1, i2, pl.ds(2 * half, 2)]

    def both_ways(u, stage, tag, block, lane):
        gather(u, stage, tag + (1,), 1, block, lane)
        gather(u, stage, tag + (3,), 3, block, lane + 1)

    def pass_on(u, stage, tag, e1, e2, lane):
        step = {0: ((e1 + 3) % 4, (e1 + 1) % 4, e2, e2), 1: (e1, e1, (e2 + 3) % 4, (e2 + 1) % 4)}[stage]
        ag[(u,) + tag + (1,)].wait_recv()
        gather(u, stage, tag + ("up",), 1, line(u, step[0], step[2], 0), lane + 2)
        ag[(u,) + tag + (3,)].wait_recv()
        gather(u, stage, tag + ("down",), 3, line(u, step[1], step[3], 1), lane + 3)

    for u in range(3):
        c1, c2, c3 = my_digits[u]
        for k in range(1, 4):
            gather(u, 2, ("a", k), k, tb[u].at[c1, c2, c3], k - 1)
    new_copy = remote(nb.at[1 - r], nbr, x_s.at[2], x_r.at[2], sibling)
    new_copy.start()
    for u in range(3):
        for k in range(1, 4):
            ag[u, "a", k].wait_recv()
        both_ways(u, 1, ("b",), line(u, 0, 0), 4)
        both_ways(u, 0, ("c", 0), line(u, 0, 0), 8)
    new_copy.wait_recv()
    kept = nb[r]
    new_out[:, :256] = jnp.where(r == 0, kept, nbr[...])
    new_out[:, 256:] = jnp.where(r == 0, nbr[...], kept)
    new_out_copy = pltpu.make_async_copy(new_out, newcb, out_s.at[2])
    new_out_copy.start()
    for u in range(3):
        pass_on(u, 1, ("b",), 0, 0, 4)
        both_ways(u, 0, ("c", 1), line(u, 0, 1), 12)
        both_ways(u, 0, ("c", 3), line(u, 0, 3), 16)
    for u in range(3):
        pass_on(u, 0, ("c", 0), 0, 0, 8)
    for u in range(3):
        ag[u, "b", "up"].wait_recv()
        ag[u, "b", "down"].wait_recv()
        both_ways(u, 0, ("c", 2), line(u, 0, 2), 20)
    for u in range(3):
        pass_on(u, 0, ("c", 1), 0, 1, 12)
        pass_on(u, 0, ("c", 3), 0, 3, 16)
    slot_copy.wait_recv()

    lane_code = (iota((SLOTS, 128), 1) + 1).astype(F32).astype(BF16)

    def take(first, steps, sem):
        for begin in range(0, len(steps), 4):
            found = []
            for j in range(begin, min(begin + 4, len(steps))):
                where = tuple(lax.rem(c + e, 4) for c, e in zip(mine, steps[j]))
                parts = []
                for u in range(3):
                    c1, c2, c3 = digits(where, u)
                    parts.append(tb[u][c1, c2, c3])
                at = pl.ds((first + j) * SLOTS, SLOTS)
                mark = jnp.concatenate([jnp.where(slot[i, at] == lane_code, one, zero) for i in range(2)], axis=0)
                got = jnp.dot(mark, jnp.concatenate(parts, axis=0), preferred_element_type=F32)
                found.append((at, got.astype(BF16)))
            for at, got in found:
                picks[r, at] = got[:SLOTS]
                psend[at] = got[SLOTS:]
        at = pl.ds(first * SLOTS, len(steps) * SLOTS)
        remote(psend.at[at], picks.at[r, at], p_s.at[sem], p_r.at[sem], sibling).start()

    def near(ez, _):
        take(ez * 9, [((0, 1, 3)[i % 3], (0, 1, 3)[i // 3], ez + ez // 2) for i in range(9)], 0)
        return 0

    lax.fori_loop(0, 3, near, 0)
    for u in range(3):
        pass_on(u, 0, ("c", 2), 0, 2, 20)

    def slot_marks(at, begin, end):
        v = vcol[at, :]
        tiles = []
        for g in range(begin // GROUP, end // GROUP):
            w = (v - (g * GS + GS // 2)).astype(BF16)
            for t in range(GS // 128):
                tiles.append(jnp.where(w == lane_slot[t], one, zero))
        return jnp.concatenate(tiles, axis=1)

    lane_slot = [(iota((BLOCK, 128), 1) + (128 * t - GS // 2)).astype(F32).astype(BF16) for t in range(GS // 128)]
    near_rows = pl.ds(0, NEAR * SLOTS)
    far_rows = pl.ds(NEAR * SLOTS, (OWNERS - NEAR) * SLOTS)
    p_copies = [remote(psend.at[at], picks.at[1 - r, at], p_s.at[i], p_r.at[i], sibling)
                for i, at in enumerate((near_rows, far_rows))]
    p_copies[0].wait_recv()

    def unpack_near(m, _):
        at = pl.ds(m * BLOCK, BLOCK)
        mark = slot_marks(at, 0, NEAR_KEPT)
        for h in range(2):
            got = jnp.dot(mark, picks[h, 0:NEAR_KEPT * SLOTS], preferred_element_type=F32)
            held[h, at] = got.astype(BF16)
        return 0

    lax.fori_loop(0, ROWS // BLOCK, unpack_near, 0)
    for u in range(3):
        for e in range(4):
            ag[u, "c", e, "up"].wait_recv()
            ag[u, "c", e, "down"].wait_recv()

    def far_z(dy, _):
        take(NEAR + dy * 4, [(i, dy, 2) for i in range(4)], 1)
        return 0

    def far_y(ez, _):
        take(NEAR + 16 + ez * 4, [(i, 2, ez + ez // 2) for i in range(4)], 1)
        return 0

    def far_x(ez, _):
        take(NEAR + 28 + ez * 3, [(2, (0, 1, 3)[i], ez + ez // 2) for i in range(3)], 1)
        return 0

    lax.fori_loop(0, 4, far_z, 0, unroll=True)
    lax.fori_loop(0, 3, far_y, 0, unroll=True)
    lax.fori_loop(0, 3, far_x, 0, unroll=True)

    outs = []
    for turn in range(2):
        h = r + turn * (1 - 2 * r)
        cols = pl.ds(pl.multiple_of(h * 256, 256), 256)
        if turn:
            p_copies[1].wait_recv()

        def unpack(m, _):
            at = pl.ds(m * BLOCK, BLOCK)
            mark = slot_marks(at, NEAR_KEPT, OWNERS)
            got = jnp.dot(mark, picks[h, NEAR_KEPT * SLOTS:], preferred_element_type=F32)
            got = got + held[h, at].astype(F32)
            out[h, at] = (rows[at, cols].astype(F32) - got).astype(BF16)
            pltpu.make_async_copy(out.at[h, at], res.at[at, cols], out_s.at[turn]).start()
            return 0

        lax.fori_loop(0, ROWS // BLOCK, unpack, 0)
        outs.append(pltpu.make_async_copy(out.at[h], res.at[:, cols], out_s.at[turn]))
    new_out_copy.wait()
    for copy in outs:
        copy.wait()

    for group in (s1_copies, sc_copies, cn_copies, s2_copies, s3_copies, ag):
        for copy in group.values():
            copy.wait_send()
    for copy in [tot_copy, cx_copy, new_copy, slot_copy] + p_copies:
        copy.wait_send()


def hand_over(new, residual):
    parts = 8

    def copy(new_in, res_in, new_out, res_out, new_buf, res_buf, sems):
        def moves(i):
            if i == parts:
                return (pltpu.make_async_copy(new_in, new_buf, sems.at[0, i]),
                        pltpu.make_async_copy(new_buf, new_out, sems.at[1, i]))
            at = pl.ds(i * (ROWS // parts), ROWS // parts)
            return (pltpu.make_async_copy(res_in.at[at], res_buf.at[at], sems.at[0, i]),
                    pltpu.make_async_copy(res_buf.at[at], res_out.at[at], sems.at[1, i]))

        pairs = [moves(i) for i in range(parts + 1)]
        for there, _ in pairs:
            there.start()
        for there, back in pairs:
            there.wait()
            back.start()
        for _, back in pairs:
            back.wait()

    anywhere = pl.BlockSpec(memory_space=pl.ANY)
    return pl.pallas_call(
        copy,
        out_shape=(jax.ShapeDtypeStruct(new.shape, new.dtype), jax.ShapeDtypeStruct(residual.shape, residual.dtype)),
        in_specs=[anywhere] * 2,
        out_specs=(anywhere, anywhere),
        scratch_shapes=[pltpu.VMEM(new.shape, new.dtype), pltpu.VMEM(residual.shape, residual.dtype),
                        pltpu.SemaphoreType.DMA((2, parts + 1))],
    )(new, residual)


def on_device(rows_in, row_codes, hot_split, codebook):
    vm = pltpu.VMEM
    dma = pltpu.SemaphoreType.DMA
    anywhere = pl.BlockSpec(memory_space=pl.ANY)
    scratch = [
        vm((ROWS, E), BF16),
        vm((LANES, 128), I32),
        vm((2, 256), I32),
        vm((KB, 256), F32),
        vm((KB // 2, E), F32),
        tuple(vm((4, 4, 4, SLOTS, w), BF16) for w in WIDTH),
        tuple(vm((4, 4, 4, PITCH, w), BF16) for w in WIDTH),
        vm((3, 16, 256), F32),
        tuple(vm((3, 4, KB, w), BF16) for w in WIDTH),
        tuple(vm((2, 2, KB, w), BF16) for w in WIDTH),
        tuple(vm((4, KB, w), F32) for w in WIDTH),
        tuple(vm((2, 4, KB, w), BF16) for w in WIDTH),
        tuple(vm((3, KB, w), BF16) for w in WIDTH),
        tuple(vm((KB, w), F32) for w in WIDTH),
        tuple(vm((3, KB, w), BF16) for w in WIDTH),
        tuple(vm((4, 4, 4, n, 256), BF16) for _, n in CUT),
        vm((4, LANES, 128), F32),
        vm((8, ROWS), F32),
        vm((ROWS, 128), F32),
        vm((3, 4, 16, 128), BF16),
        vm((3, 4, 16, 128), BF16),
        vm((4, 16, 128), F32),
        vm((4, 16, 128), F32),
        vm((16, 128), F32),
        vm((3, 16, 128), F32),
        vm((16, 128), F32),
        vm((3, 16, 128), F32),
        vm((8, 128), F32),
        vm((8, 128), F32),
        vm((2, KB, 256), F32),
        vm((KB, 256), F32),
        vm((2, 64, 256), F32),
        vm((64, 256), F32),
        vm((2, OWNERS * SLOTS, 128), BF16),
        vm((2, OWNERS * SLOTS, 256), BF16),
        vm((OWNERS * SLOTS, 256), BF16),
        vm((2, ROWS, 256), BF16),
        vm((2, ROWS, 256), BF16),
        dma((4,)), dma((3,)),
        dma((3, 6)), dma((3, 6)),
        dma((3, 3, 4)), dma((3, 3, 4)),
        dma((3, 4)), dma((3, 4)),
        dma((3, 4)), dma((3, 4)),
        dma((3, 24)), dma((3, 24)),
        dma((4,)), dma((4,)),
        dma((2,)), dma((2,)),
    ]
    new, residual = pl.pallas_call(
        kernel,
        out_shape=(jax.ShapeDtypeStruct((KB // 2, E), F32), jax.ShapeDtypeStruct((ROWS, E), BF16)),
        in_specs=[anywhere] * 4,
        out_specs=(anywhere, anywhere),
        scratch_shapes=scratch,
        compiler_params=pltpu.CompilerParams(collective_id=0, has_side_effects=True,
                                             vmem_limit_bytes=56 * 2**20),
    )(rows_in, row_codes.reshape(LANES, 128), hot_split.T, codebook)
    return hand_over(new, residual)


def solution(mesh):
    return jax.shard_map(
        on_device,
        mesh=mesh,
        in_specs=(P(("dp", "rep"), None), P(("dp", "rep")), P(), P("dp", None)),
        out_specs=(P(("dp", "rep"), None), P(("dp", "rep"), None)),
        check_vma=False,
    )
```
